128 devices in a mesh: clip: 4 (over y), space: 32 (over x, z, core).
Axes of the slice: x: 4, y: 4, z: 4, core: 2. Of those that a mesh axis runs over, the one named last changes fastest.
Arguments:
- frames: bfloat16 [4, 1024, 256, 256], P('clip', 'space'), may hold values from -6 to 6
- tail_frame: bfloat16 [1024, 256, 256], P('space'), may hold values from -6 to 6
- cotangent: bfloat16 [4, 1024, 2, 81, 256], P('clip', 'space'), may hold values from -6 to 6
- window_base: int32 [4, 1024, 2, 2, 256], P('clip', 'space'), may hold values from 4 to 10
- window_frac: bfloat16 [4, 1024, 2, 2, 256], P('clip', 'space'), may hold values from 0 to 1
- fine_owner: int32 [4, 1024, 1], P('clip'), may hold values from 0 to 31; in each aligned block of 32 rows (0 to 31, 32 to 63, ..., all dimensions but the last counted through in order) at most 2 rows name the same one
- fine_local: int32 [4, 1024], P('clip'), may hold values from 0 to 31
- coarse_owner: int32 [4, 1024, 1], P('clip'), may hold values from 0 to 31; in each aligned block of 32 rows (0 to 31, 32 to 63, ..., all dimensions but the last counted through in order) at most 2 rows name the same one
- coarse_block: int32 [4, 1024], P('clip'), may hold values from 0 to 1
Outputs:
- grad_first: bfloat16 [4, 1024, 256, 256], P('clip', 'space')
- grad_second: bfloat16 [4, 1024, 256, 256], P('clip', 'space')
The draws below stay inside these ranges and needn't reach their ends.
Inputs may be any that keep to these rules, and one draw needn't show every extreme that they name: `fine_owner`: among the 32 query tiles of one device no device index is named more than 2 times, a bound that some block reaches. `coarse_owner`: among the 32 query tiles of one device no device index is named more than 2 times, a bound that some block reaches. `window_base`: every window lies inside its target tile.
All inputs are finite; a program needn't handle non-finite values.
Results may differ from the reference program's by a relative error of at most 0.0085.
Values may be sent and summed in bfloat16 or wider, within the bound.
A program may use at most 256 MiB of HBM per device.

```python
import math
import jax
import jax.numpy as jnp
import numpy as np
from jax import lax

C = 256
TS = 16
WIN = 9
POOL = 4
LEVELS = 2
BLOCKS_DEV = 2
PIX = 256
TILES_DEV = 32
TILES = 1024
MOST = 2
PAIRS = 4
N_CLIP = 4
N_SPACE = 32


def place_ends(result, own_key, smallest, top_value):
    shape = result.shape
    index_at = [jax.random.randint(jax.random.fold_in(own_key, axis), (), 0, shape[axis]) for axis in range(len(shape))]
    result = result.at[tuple(index_at)].set(smallest)
    longest = shape.index(max(shape))
    index_at[longest] = (index_at[longest] + 1) % shape[longest]
    return result.at[tuple(index_at)].set(top_value)


def levels(key, shape, cuts, smallest, high):
    factor_of, own = 1.0, jax.random.fold_in(key, 6)
    for position, blocks in cuts:
        draws = jnp.exp(jax.random.uniform(jax.random.fold_in(own, position), (blocks,), jnp.float32, smallest / len(cuts), high / len(cuts)))
        factor_of = factor_of * jnp.repeat(draws, shape[position] // blocks).reshape([-1 if axis == position else 1 for axis in range(len(shape))])
    return factor_of


def routed_block(rng, own, number, rows, count, top, limit, slope):
    sequence = jax.random.permutation(rng, count)
    packed, common = load_shares(count, rows * top, limit, slope, True), load_shares(count, rows * top, limit, slope, False)
    places = jnp.arange(count)

    def named(lengths, rotation):
        used = int((lengths > 0).sum())
        fixed = max(1, used // 4)
        passed = fixed + (places - fixed + rotation * (used - fixed)) % max(1, count - fixed)
        return jnp.zeros((count,), jnp.int32).at[sequence[jnp.where(places < fixed, places, passed)]].set(jnp.asarray(lengths, jnp.int32))

    lengths = jnp.where(number % 4 == 0, named(packed, number // 4), named(common, number - number // 4 - 1))
    mixed = jax.random.permutation(jax.random.fold_in(own, 3), count)
    donor, sink = mixed[0:count // 2 * 2:2], mixed[1:count // 2 * 2:2]
    slack = jnp.minimum(lengths[donor] - 1, limit - lengths[sink]) // 2
    slack = jnp.where((donor == sequence[0]) | (sink == sequence[0]) | (lengths[sink] == 0), 0, jnp.maximum(slack, 0))
    passed = jax.random.randint(jax.random.fold_in(own, 4), (count // 2,), 0, 1 << 20) % (slack + 1)
    lengths = lengths.at[donor].add(-passed).at[sink].add(passed)
    labels = jnp.searchsorted(jnp.cumsum(lengths), jnp.arange(rows * top), side="right").astype(jnp.int32)
    grid = labels.reshape(top, rows).T
    grid = grid[jax.random.permutation(jax.random.fold_in(own, 1), rows)]
    rotation = jax.random.randint(jax.random.fold_in(own, 2), (rows, 1), 0, top)
    return jnp.take_along_axis(grid, (jnp.arange(top)[None, :] + rotation) % top, axis=1)


def load_shares(amount, total, bound, lean, full):
    loads = [(1 << 20) // math.isqrt(rank ** lean) + 1 for rank in range(1, amount + 1)]
    largest = bound if full else min(bound, max(-(-total // amount), total * loads[0] // sum(loads)))
    least = 1 if total - largest >= amount - 1 else 0
    counts, spare = [largest] + [least] * (amount - 1), total - largest - least * (amount - 1)
    while spare > 0:
        free = [i for i in range(1, amount) if counts[i] < largest] or [i for i in range(1, amount) if counts[i] < bound]
        pool, budget = sum([loads[i] for i in free]), spare
        for i in free:
            extra = min(bound - counts[i], max(1, budget * loads[i] // pool), spare)
            counts[i] = counts[i] + extra
            spare = spare - extra
    return np.array(counts)


def bell_draw(stream_key, extent, scale, bound, shards=(), kind=jnp.bfloat16):
    gain = levels(stream_key, extent, shards, -0.22, 0.18) if shards else 1.0
    entries = jax.random.normal(stream_key, extent, jnp.float32) * scale * gain
    return jnp.minimum(jnp.maximum(entries, -bound), bound).astype(kind)


def setup_inputs(seed: int = 0) -> dict:
    arg_keys = jax.random.split(jax.random.key(seed), 10)
    frames = bell_draw(arg_keys[0], (PAIRS, TILES, PIX, C), 1.0, 6.0, ((0, 4), (1, 32)))
    tail_frame = bell_draw(arg_keys[1], (TILES, PIX, C), 1.0, 6.0, ((0, 32),))
    cotangent = bell_draw(arg_keys[2], (PAIRS, TILES, LEVELS, WIN * WIN, PIX), 1.0, 6.0, ((0, 4), (1, 32)))
    window_base = place_ends(jax.random.randint(arg_keys[3], (PAIRS, TILES, LEVELS, 2, PIX), WIN // 2, TS - WIN // 2 - 1), jax.random.fold_in(arg_keys[3], 1), WIN // 2, (TS - WIN // 2 - 1) - 1).astype(jnp.int32)
    window_frac = jnp.clip(1.0 * jax.random.uniform(arg_keys[4], (PAIRS, TILES, LEVELS, 2, PIX), jnp.float32) ** levels(arg_keys[4], (PAIRS, TILES, LEVELS, 2, PIX), ((0, 4), (1, 32)), -0.2, 0.2), 0.0, 1.0).astype(jnp.bfloat16)
    fine_owner_keys = jax.random.split(jax.random.fold_in(arg_keys[5], 1), PAIRS * TILES // TILES_DEV)
    fine_owner_turns = jax.random.permutation(jax.random.fold_in(arg_keys[5], 3), PAIRS * TILES // TILES_DEV)
    fine_owner = jax.vmap(lambda own, number: routed_block(jax.random.fold_in(arg_keys[5], 2), own, number, TILES_DEV, N_SPACE, 1, MOST, 2))(fine_owner_keys, fine_owner_turns).reshape((PAIRS, TILES, 1))
    fine_local = place_ends(jax.random.randint(arg_keys[6], (PAIRS, TILES), 0, TILES_DEV), jax.random.fold_in(arg_keys[6], 1), 0, TILES_DEV - 1).astype(jnp.int32)
    coarse_owner_keys = jax.random.split(jax.random.fold_in(arg_keys[7], 1), PAIRS * TILES // TILES_DEV)
    coarse_owner_turns = jax.random.permutation(jax.random.fold_in(arg_keys[7], 3), PAIRS * TILES // TILES_DEV)
    coarse_owner = jax.vmap(lambda own, number: routed_block(jax.random.fold_in(arg_keys[7], 2), own, number, TILES_DEV, N_SPACE, 1, MOST, 2))(coarse_owner_keys, coarse_owner_turns).reshape((PAIRS, TILES, 1))
    coarse_block = place_ends(jax.random.randint(arg_keys[8], (PAIRS, TILES), 0, BLOCKS_DEV), jax.random.fold_in(arg_keys[8], 1), 0, BLOCKS_DEV - 1).astype(jnp.int32)
    return dict(frames=frames, tail_frame=tail_frame, cotangent=cotangent, window_base=window_base, window_frac=window_frac, fine_owner=fine_owner, fine_local=fine_local, coarse_owner=coarse_owner, coarse_block=coarse_block)


def window_weights(base, fraction, tile_side, window_side):
    radius = window_side // 2
    offsets = jnp.arange(window_side, dtype=jnp.int32) - radius
    window_start = base[:, None, None, :] + offsets[None, :, None, None]
    column = jnp.arange(tile_side, dtype=jnp.int32)[None, None, :, None]
    at_lower = (column == window_start).astype(jnp.float32)
    at_upper = (column == window_start + 1).astype(jnp.float32)
    share = fraction[:, None, None, :]
    return (1.0 - share) * at_lower + share * at_upper

def window_grad(cotan, base, fraction):
    query_count = cotan.shape[0]
    pixels = cotan.shape[-1]
    tile_side = math.isqrt(pixels)
    window_side = math.isqrt(cotan.shape[1])
    values = cotan.astype(jnp.float32).reshape(query_count, window_side, window_side, pixels)
    cols_weight = window_weights(base[:, 0], fraction[:, 0].astype(jnp.float32), tile_side, window_side)
    rows_weight = window_weights(base[:, 1], fraction[:, 1].astype(jnp.float32), tile_side, window_side)
    partial_value = jnp.zeros((query_count, window_side, tile_side, pixels), jnp.float32)
    for shift_index in range(window_side):
        partial_value = partial_value + values[:, :, shift_index, None, :] * cols_weight[:, shift_index, None, :, :]
    window_map = jnp.zeros((query_count, tile_side, tile_side, pixels), jnp.float32)
    for shift_index in range(window_side):
        window_map = window_map + rows_weight[:, shift_index, :, None, :] * partial_value[:, shift_index, None, :, :]
    return window_map.reshape(query_count, pixels, pixels).astype(jnp.bfloat16)

def first_rows(target):
    matches = target[:, None] == target[None, :]
    ordinal = jnp.arange(target.shape[0])
    earlier = matches & (ordinal[None, :] < ordinal[:, None])
    leading = jnp.logical_not(jnp.any(earlier, axis=1))
    return (matches & leading[:, None]).astype(jnp.float32)

def combine(target, terms):
    return jnp.einsum('ab,bjc->ajc', first_rows(target), terms, precision=lax.Precision.HIGHEST)

def correlate(window_map, tiles, queries, norm_scale):
    grid_wide = window_map.astype(jnp.float32)
    query_grad = jnp.einsum('qji,qjc->qic', grid_wide, tiles.astype(jnp.float32)) * norm_scale
    toward = jnp.einsum('qji,qic->qjc', grid_wide, queries.astype(jnp.float32)) * norm_scale
    return (query_grad, toward)

def pooled_map(frame):
    tile_count, pixels, channels = frame.shape
    tile_side = math.isqrt(pixels)
    coarse_side = tile_side // POOL
    blocks = tile_count // (POOL * POOL)
    pieces = frame.reshape(blocks, POOL, POOL, coarse_side, POOL, coarse_side, POOL, channels)
    averages = lax.optimization_barrier(jnp.sum(pieces, axis=(4, 6), dtype=jnp.float32)) / (POOL * POOL)
    return averages.transpose(0, 1, 3, 2, 4, 5).reshape(blocks, pixels, channels).astype(jnp.bfloat16)

def spread_back(grads):
    blocks, pixels, channels = grads.shape
    tile_side = math.isqrt(pixels)
    coarse_side = tile_side // POOL
    pieces = grads.reshape(blocks, POOL, coarse_side, POOL, coarse_side, channels).transpose(0, 1, 3, 2, 4, 5)
    expanded = jnp.broadcast_to(pieces[:, :, :, :, None, :, None, :], (blocks, POOL, POOL, coarse_side, POOL, coarse_side, POOL, channels)) / (POOL * POOL)
    return expanded.reshape(blocks * POOL * POOL, pixels, channels)

def pair_grads(first_tiles, second_tiles, cotan, base, fraction, fine_ids, coarse_ids):
    tile_count, pixels, channels = first_tiles.shape
    norm_scale = 1.0 / math.sqrt(channels)
    pooled = pooled_map(second_tiles)
    blocks_all = pooled.shape[0]

    def block_step(totals, block_items):
        fine_total, coarse_total = totals
        queries, cot_block, base_block, frac_block, fine_block, coarse_block_ids = block_items
        fine_map = window_grad(cot_block[:, 0], base_block[:, 0], frac_block[:, 0])
        fine_back, fine_toward = correlate(fine_map, second_tiles[fine_block], queries, norm_scale)
        fine_back = lax.optimization_barrier(fine_back.astype(jnp.bfloat16)).astype(jnp.float32)
        fine_part = lax.optimization_barrier(combine(fine_block, fine_toward).astype(jnp.bfloat16)).astype(jnp.float32)
        fine_total = fine_total.at[fine_block].add(fine_part)
        coarse_map = window_grad(cot_block[:, 1], base_block[:, 1], frac_block[:, 1])
        coarse_back, coarse_toward = correlate(coarse_map, pooled[coarse_block_ids], queries, norm_scale)
        coarse_part = lax.optimization_barrier(combine(coarse_block_ids, coarse_toward).astype(jnp.bfloat16)).astype(jnp.float32)
        coarse_total = coarse_total.at[coarse_block_ids].add(coarse_part)
        return ((fine_total, coarse_total), (fine_back + coarse_back).astype(jnp.bfloat16))
    per_device = tile_count // N_SPACE
    block_items = (first_tiles.reshape((N_SPACE, per_device) + first_tiles.shape[1:]), cotan.reshape((N_SPACE, per_device) + cotan.shape[1:]), base.reshape((N_SPACE, per_device) + base.shape[1:]), fraction.reshape((N_SPACE, per_device) + fraction.shape[1:]), fine_ids.reshape(N_SPACE, per_device), coarse_ids.reshape(N_SPACE, per_device))
    start_totals = (jnp.zeros((tile_count, pixels, channels), jnp.float32), jnp.zeros((blocks_all, pixels, channels), jnp.float32))
    totals, first_grads = lax.scan(block_step, start_totals, block_items)
    fine_total, coarse_total = totals
    second_grad = (fine_total + spread_back(coarse_total)).astype(jnp.bfloat16)
    return (first_grads.reshape(tile_count, pixels, channels), second_grad)

def reference(frames, tail_frame, cotangent, window_base, window_frac, fine_owner, fine_local, coarse_owner, coarse_block):
    firsts = []
    seconds = []
    for pair_index in range(N_CLIP):
        if pair_index + 1 < N_CLIP:
            second_tiles = frames[pair_index + 1]
        else:
            second_tiles = tail_frame
        fine_ids = (fine_owner[pair_index, :, 0] * TILES_DEV + fine_local[pair_index]).astype(jnp.int32)
        coarse_ids = (coarse_owner[pair_index, :, 0] * BLOCKS_DEV + coarse_block[pair_index]).astype(jnp.int32)
        first_grad, second_grad = pair_grads(frames[pair_index], second_tiles, cotangent[pair_index], window_base[pair_index], window_frac[pair_index], fine_ids, coarse_ids)
        firsts.append(first_grad)
        seconds.append(second_grad)
    return (jnp.stack(firsts), jnp.stack(seconds))
```

```python
import functools
import math

import jax
import jax.numpy as jnp
import numpy as np
from jax import lax
from jax.experimental import pallas as pl
from jax.experimental.pallas import tpu as pltpu
from jax.sharding import PartitionSpec as P

MESH = pl.DeviceIdType.MESH
POOL = 4
SIDE = 16
WIN = 9
PIX = 256
HALF = PIX // 2
NX, NZ, NC = 4, 4, 2
BLK = 2
TILES = 32
SLOTS = 2 * TILES
F32 = jnp.float32
BF16 = jnp.bfloat16


def placement():
    spread = np.zeros((2 * WIN * SIDE, WIN * WIN), np.float32)
    for a in range(WIN):
        for k in range(WIN):
            spread[a * SIDE + k, a * WIN + k] = 1
            spread[WIN * SIDE + a * SIDE + k + 1, a * WIN + k] = 1
    return spread


def pool_rows():
    rows = np.zeros((SIDE, PIX), np.float32)
    for y in range(SIDE):
        for x in range(SIDE):
            rows[(y // POOL) * POOL + x // POOL, y * SIDE + x] = 1
    return rows


def block_rows():
    rows = np.zeros((PIX, PIX), np.float32)
    for ty in range(4):
        for tx in range(4):
            for a in range(4):
                for b in range(4):
                    rows[(ty * 4 + a) * 16 + tx * 4 + b, (ty * 4 + tx) * 16 + a * 4 + b] = 1
    return rows


def dot(a, b):
    return jnp.dot(a, b, preferred_element_type=F32)


def window_map(spread, cot, base, frac):
    placed = dot(spread, cot)
    rows = WIN * SIDE
    fx = frac[0:1].astype(F32)
    fy = frac[1:2].astype(F32)
    shape = (SIDE, PIX)
    ox = jnp.broadcast_to(base[0:1] - WIN // 2, shape)
    oy = jnp.broadcast_to(base[1:2] - WIN // 2, shape)
    across = (1.0 - fx) * placed[:rows] + fx * placed[rows:]
    groups = []
    for y in range(WIN + 1):
        value = None
        if y < WIN:
            value = (1.0 - fy) * across[y * SIDE : (y + 1) * SIDE]
        if y > 0:
            below = fy * across[(y - 1) * SIDE : y * SIDE]
            value = below if value is None else value + below
        groups.append(value)
    for step in (1, 2, 4):
        chosen = (ox & step) != 0
        groups = [jnp.where(chosen, pltpu.roll(g, step, 0), g) for g in groups]
    zero = jnp.zeros(shape, F32)
    for step in (1, 2, 4):
        chosen = (oy & step) != 0
        count = min(SIDE, len(groups) + step)
        groups = [
            jnp.where(
                chosen,
                groups[y - step] if y >= step else zero,
                groups[y] if y < len(groups) else zero,
            )
            for y in range(count)
        ]
    return jnp.concatenate(groups, axis=0).astype(BF16)


def prep_kernel(
    slot_ref, spread_ref, pool_ref, perm_ref, cot_ref, base_ref, frac_ref, frame_ref, tail_ref,
    fine_ref, coarse_ref, ret_ref, terms_ref, pooled_ref, raw
):
    step = pl.program_id(0)
    scale = 1.0 / 16.0
    frame = frame_ref[0]
    fine = window_map(spread_ref[...], cot_ref[0, 0], base_ref[0, 0], frac_ref[0, 0])
    fine_ref[0] = fine
    ret_ref[0] = (dot(fine, frame) * scale).astype(BF16)
    coarse = window_map(spread_ref[...], cot_ref[0, 1], base_ref[0, 1], frac_ref[0, 1])
    coarse_ref[0] = coarse
    terms_ref[0] = (dot(coarse, frame) * scale).astype(BF16)
    rows = pl.ds(pl.multiple_of((step % 16) * SIDE, SIDE), SIDE)
    block = step // 16
    raw[0, block, rows, :] = (dot(pool_ref[...], frame) * scale).astype(BF16)
    raw[1, block, rows, :] = (dot(pool_ref[...], tail_ref[0]) * scale).astype(BF16)

    @pl.when(step == TILES - 1)
    def _():
        for which in range(2):
            for b in range(BLK):
                pooled_ref[which, b] = dot(perm_ref[...], raw[which, b]).astype(BF16)


def prep(slots, cot, base, frac, frames, tail):
    tile = lambda q, s: (q, 0, 0)
    whole = lambda q, s: (0, 0)
    four = lambda q, s: (q, 0, 0, 0)
    one = (1, PIX, PIX)
    out = jax.ShapeDtypeStruct((TILES, PIX, PIX), BF16)
    return pl.pallas_call(
        prep_kernel,
        grid_spec=pltpu.PrefetchScalarGridSpec(
            num_scalar_prefetch=1,
            grid=(TILES,),
            in_specs=[
                pl.BlockSpec((2 * WIN * SIDE, WIN * WIN), whole),
                pl.BlockSpec((SIDE, PIX), whole),
                pl.BlockSpec((PIX, PIX), whole),
                pl.BlockSpec((1, 2, WIN * WIN, PIX), four),
                pl.BlockSpec((1, 2, 2, PIX), four),
                pl.BlockSpec((1, 2, 2, PIX), four),
                pl.BlockSpec(one, tile),
                pl.BlockSpec(one, tile),
            ],
            out_specs=[
                pl.BlockSpec(one, tile),
                pl.BlockSpec(one, tile),
                pl.BlockSpec(one, lambda q, s: (s[q], 0, 0)),
                pl.BlockSpec(one, tile),
                pl.BlockSpec((2, BLK, PIX, PIX), lambda q, s: (0, 0, 0, 0)),
            ],
            scratch_shapes=[pltpu.VMEM((2, BLK, PIX, PIX), BF16)],
        ),
        out_shape=[out, out, jax.ShapeDtypeStruct((SLOTS, PIX, PIX), BF16), out,
                   jax.ShapeDtypeStruct((2, BLK, PIX, PIX), BF16)],
        compiler_params=pltpu.CompilerParams(vmem_limit_bytes=40 * 2**20),
        name="prep",
    )(slots, jnp.asarray(placement(), BF16), jnp.asarray(pool_rows(), BF16),
      jnp.asarray(block_rows(), BF16), cot, base, frac, frames, tail)


def exchange_kernel(
    served_ref, pick_a, pick_b, frames, tail, ret, terms, pooled,
    got, back, every, coarse_ref, ret_a, ret_b, get_a, get_b,
    tiles, fetch, own, partial, sibling, pbuf,
    red_a, red_b, mid_a, mid_b, last_a, last_b, coarse,
    send, recv, local
):
    clip = lax.axis_index("clip")
    space = lax.axis_index("space")
    x = space // (NZ * NC)
    z = (space // NC) % NZ
    c = space % NC
    counts = {"remote": 0, "local": 0}

    def along_x(d, core=0):
        return (clip, (((x + d) % NX) * NZ + z) * NC + (c + core) % NC)

    def along_z(d, core=0):
        return (clip, (x * NZ + (z + d) % NZ) * NC + (c + core) % NC)

    def remote(src, dst, device):
        n = counts["remote"]
        counts["remote"] += 1
        return pltpu.make_async_remote_copy(
            src_ref=src, dst_ref=dst, send_sem=send.at[n], recv_sem=recv.at[n],
            device_id=device, device_id_type=MESH)

    def here(src, dst):
        n = counts["local"]
        counts["local"] += 1
        return pltpu.make_async_copy(src, dst, local.at[n])

    def start(copies):
        for copy in copies:
            copy.start()
        return copies

    def arrive(copies):
        for copy in copies:
            copy.wait_recv()

    barrier = pltpu.get_barrier_semaphore()
    greeted = [along_x(d, k) for d in range(1, NX) for k in range(NC)]
    greeted += [along_z(d, k) for d in range(1, NZ) for k in range(NC)]
    greeted += [along_x(0, 1), ((clip + 1) % 4, space)]
    for device in greeted:
        pl.semaphore_signal(barrier, inc=1, device_id=device, device_id_type=MESH)
    pl.semaphore_wait(barrier, len(greeted))

    sent = []
    at_end = clip == 3
    below = ((clip + 3) % 4, space)
    move_pool = remote(pooled.at[0], pbuf, below)
    move_tiles = remote(frames, tiles, below)
    end_pool = here(pooled.at[1], pbuf)
    end_tiles = here(tail, tiles)

    @pl.when(clip > 0)
    def _():
        move_pool.start()
        move_tiles.start()

    @pl.when(at_end)
    def _():
        end_pool.start()
        end_tiles.start()

    load_terms = start([here(terms, own.at[pl.ds(0, TILES)])])

    keep_a = start([here(ret.at[0, x], ret_a.at[:, :, x])])
    keep_b = start([here(ret.at[1, z], ret_b.at[:, :, z])])
    ret_a1 = start([remote(ret.at[0, (x + d) % NX], ret_a.at[:, :, x], along_x(d)) for d in range(1, NX)])
    ret_b1 = start([remote(ret.at[1, (z + d) % NZ], ret_b.at[:, :, z], along_z(d)) for d in range(1, NZ)])
    sent += ret_a1 + ret_b1

    own[TILES] = jnp.zeros((PIX, PIX), BF16)
    for copy in load_terms:
        copy.wait()

    def picked(n):
        first = own[pick_a[n]].astype(F32)
        return (first + own[pick_b[n]].astype(F32)).astype(BF16)

    def fill(which, core):
        def one(n, carry):
            partial[which, n // (NZ * BLK), (n // BLK) % NZ, n % BLK] = picked(core * TILES + n)
            return carry
        lax.fori_loop(0, TILES, one, 0)

    fill(1, 1 - c)
    share = start([remote(partial.at[1], sibling, along_x(0, 1))])
    sent += share
    fill(0, c)

    @pl.when(at_end)
    def _():
        end_pool.wait()

    @pl.when(clip < 3)
    def _():
        move_pool.wait_recv()

    top, bottom = pl.ds(0, HALF), pl.ds(HALF, HALF)
    keep_pool = start([here(pbuf, every.at[c, x, z])])
    pool_a1 = start([remote(pbuf.at[:, top], every.at[c, x, z, :, top], along_x(d)) for d in range(1, NX)])
    pool_b1 = start([remote(pbuf.at[:, bottom], every.at[c, x, z, :, bottom], along_z(d)) for d in range(1, NZ)])
    sent += pool_a1 + pool_b1

    arrive(share)

    def join(n, carry):
        at = (n // (NZ * BLK), (n // BLK) % NZ, n % BLK)
        mine = partial[(0, *at)].astype(F32)
        partial[(0, *at)] = (mine + sibling[at].astype(F32)).astype(BF16)
        return carry

    lax.fori_loop(0, TILES, join, 0)
    mine = partial.at[0]
    red_a1 = start([remote(mine.at[:, (z + d) % NZ, :, top], red_a.at[z], along_z(d)) for d in range(1, NZ)])
    red_b1 = start([remote(mine.at[(x + d) % NX, :, :, bottom], red_b.at[x], along_x(d)) for d in range(1, NX)])
    sent += red_a1 + red_b1

    def store_own_a(n, carry):
        red_a[z, n // BLK, n % BLK] = partial[0, n // BLK, z, n % BLK, top]
        red_b[x, n // BLK, n % BLK] = partial[0, x, n // BLK, n % BLK, bottom]
        return carry

    lax.fori_loop(0, NX * BLK, store_own_a, 0)

    for copy in keep_pool:
        copy.wait()
    arrive(pool_a1)
    pool_a2 = start([remote(every.at[c, :, z, :, top], every.at[c, :, z, :, top], along_z(d)) for d in range(1, NZ)])
    arrive(pool_b1)
    pool_b2 = start([remote(every.at[c, x, :, :, bottom], every.at[c, x, :, :, bottom], along_x(d)) for d in range(1, NX)])
    sent += pool_a2 + pool_b2

    def total(buffer, at):
        value = buffer[(0, *at)].astype(F32)
        for n in range(1, 4):
            value = value + buffer[(n, *at)].astype(F32)
        return value

    arrive(red_a1)
    arrive(red_b1)

    def middle(n, carry):
        at = (n // BLK, n % BLK)
        mid_a[at] = total(red_a, at).astype(BF16)
        mid_b[at] = total(red_b, at).astype(BF16)
        return carry

    lax.fori_loop(0, NX * BLK, middle, 0)
    red_a2 = start([remote(mid_a.at[(x + d) % NX], last_a.at[x], along_x(d)) for d in range(1, NX)])
    red_b2 = start([remote(mid_b.at[(z + d) % NZ], last_b.at[z], along_z(d)) for d in range(1, NZ)])
    sent += red_a2 + red_b2
    last_a[x] = mid_a[x]
    last_b[z] = mid_b[z]

    keep_a[0].wait()
    arrive(ret_a1)
    others = [(d, k) for d in range(NZ) for k in range(NC) if d or k]
    ret_a2 = start([remote(ret_a.at[(z + d) % NZ, (c + k) % NC], back.at[0, z, c], along_z(d, k)) for d, k in others])
    keep_b[0].wait()
    arrive(ret_b1)
    ret_b2 = start([remote(ret_b.at[(x + d) % NX, (c + k) % NC], back.at[1, x, c], along_x(d, k)) for d, k in others])
    sent += ret_a2 + ret_b2
    stay = start([here(ret_a.at[z, c], back.at[0, z, c]), here(ret_b.at[x, c], back.at[1, x, c])])

    @pl.when(at_end)
    def _():
        end_tiles.wait()

    @pl.when(clip < 3)
    def _():
        move_tiles.wait_recv()

    def serve(n, carry):
        fetch[n // TILES, (n // (NZ * NC)) % NX, (n // NC) % NZ, n % NC] = tiles[served_ref[n]]
        return carry

    lax.fori_loop(0, SLOTS, serve, 0)
    keep_fa = start([here(fetch.at[0, x], get_a.at[:, :, x])])
    keep_fb = start([here(fetch.at[1, z], get_b.at[:, :, z])])
    get_a1 = start([remote(fetch.at[0, (x + d) % NX], get_a.at[:, :, x], along_x(d)) for d in range(1, NX)])
    get_b1 = start([remote(fetch.at[1, (z + d) % NZ], get_b.at[:, :, z], along_z(d)) for d in range(1, NZ)])
    sent += get_a1 + get_b1

    arrive(pool_a2)
    arrive(pool_b2)
    pool_3 = start([remote(every.at[c], every.at[c], along_x(0, 1))])
    sent += pool_3

    arrive(red_a2)
    arrive(red_b2)
    for b in range(BLK):
        coarse[b, top] = total(last_a, (b,)).astype(BF16)
        coarse[b, bottom] = total(last_b, (b,)).astype(BF16)
    put_coarse = start([here(coarse, coarse_ref)])

    keep_fa[0].wait()
    arrive(get_a1)
    get_a2 = start([remote(get_a.at[(z + d) % NZ, (c + k) % NC], got.at[0, z, c], along_z(d, k)) for d, k in others])
    keep_fb[0].wait()
    arrive(get_b1)
    get_b2 = start([remote(get_b.at[(x + d) % NX, (c + k) % NC], got.at[1, x, c], along_x(d, k)) for d, k in others])
    sent += get_a2 + get_b2
    stay += start([here(get_a.at[z, c], got.at[0, z, c]), here(get_b.at[x, c], got.at[1, x, c])])

    arrive(ret_a2)
    arrive(ret_b2)
    arrive(pool_3)
    arrive(get_a2)
    arrive(get_b2)
    for copy in stay + put_coarse:
        copy.wait()
    for copy in sent:
        copy.wait_send()

    @pl.when(clip > 0)
    def _():
        move_pool.wait_send()
        move_tiles.wait_send()


def exchange(served, pick_a, pick_b, frames, tail, ret, terms, pooled):
    smem = pl.BlockSpec(memory_space=pltpu.SMEM)
    hbm = pl.BlockSpec(memory_space=pl.ANY)
    tile = (PIX, PIX)
    shape = lambda *s: jax.ShapeDtypeStruct(s + tile, BF16)
    half = lambda *s: pltpu.VMEM(s + (HALF, PIX), BF16)
    full = lambda *s: pltpu.VMEM(s + tile, BF16)
    outs = pl.pallas_call(
        exchange_kernel,
        in_specs=[smem] * 3 + [hbm] * 5,
        out_specs=[hbm] * 8,
        out_shape=[
            shape(2, 4, NC, 4), shape(2, 4, NC, 4), shape(NC, NX, NZ, BLK), shape(BLK),
            shape(NZ, NC, NX), shape(NX, NC, NZ), shape(NZ, NC, NX), shape(NX, NC, NZ),
        ],
        scratch_shapes=[
            full(TILES), full(2, 4, 4, NC), full(TILES + 1), full(2, NX, NZ, BLK),
            full(NX, NZ, BLK), full(BLK),
            half(NZ, NX, BLK), half(NX, NZ, BLK), half(NX, BLK), half(NZ, BLK),
            half(NX, BLK), half(NZ, BLK), full(BLK),
            pltpu.SemaphoreType.DMA((80,)), pltpu.SemaphoreType.DMA((80,)),
            pltpu.SemaphoreType.DMA((16,)),
        ],
        compiler_params=pltpu.CompilerParams(
            collective_id=0, has_side_effects=True, vmem_limit_bytes=56 * 2**20),
        name="exchange",
    )(served, pick_a, pick_b, frames, tail, ret.reshape(2, 4, 4, NC, PIX, PIX), terms, pooled)
    return outs[:4]


def finish_kernel(
    slot_ref, ctile_ref, first_ref, order_ref, perm_ref, widen_ref,
    fine_ref, coarse_ref, got_ref, every_ref, back_ref, csum_ref,
    grad_a, grad_b, raw
):
    step = pl.program_id(0)
    scale = 1.0 / 16.0
    flip = (((0,), (0,)), ((), ()))

    @pl.when(step == 0)
    def _():
        for b in range(BLK):
            raw[b] = lax.dot_general(perm_ref[...], csum_ref[b], flip, preferred_element_type=F32).astype(BF16)

    fine = lax.dot_general(fine_ref[0], got_ref[0], flip, preferred_element_type=F32) * scale
    coarse = lax.dot_general(coarse_ref[0], every_ref[0], flip, preferred_element_type=F32) * scale
    grad_a[0] = (fine.astype(BF16).astype(F32) + coarse).astype(BF16)

    rows = pl.ds(pl.multiple_of((step % 16) * SIDE, SIDE), SIDE)
    spread = dot(widen_ref[...], raw[step // 16, rows, :]) * scale

    def add(n, value):
        return value + back_ref[order_ref[n]].astype(F32)

    grad_b[0] = lax.fori_loop(first_ref[step], first_ref[step + 1], add, spread).astype(BF16)


def finish(slots, ctile, first, order, fine, coarse, got, every, back, csum):
    one = (1, PIX, PIX)
    tile = lambda q, *s: (q, 0, 0)
    whole = lambda q, *s: (0, 0)
    out = jax.ShapeDtypeStruct((TILES, PIX, PIX), BF16)
    return pl.pallas_call(
        finish_kernel,
        grid_spec=pltpu.PrefetchScalarGridSpec(
            num_scalar_prefetch=4,
            grid=(TILES,),
            in_specs=[
                pl.BlockSpec((PIX, PIX), whole),
                pl.BlockSpec((PIX, SIDE), whole),
                pl.BlockSpec(one, tile),
                pl.BlockSpec(one, tile),
                pl.BlockSpec(one, lambda q, s, ct, f, o: (s[q], 0, 0)),
                pl.BlockSpec(one, lambda q, s, ct, f, o: (ct[q], 0, 0)),
                pl.BlockSpec((SLOTS, PIX, PIX), lambda q, *s: (0, 0, 0), pipeline_mode=pl.Buffered(1)),
                pl.BlockSpec((BLK, PIX, PIX), lambda q, *s: (0, 0, 0)),
            ],
            out_specs=[pl.BlockSpec(one, tile), pl.BlockSpec(one, tile)],
            scratch_shapes=[pltpu.VMEM((BLK, PIX, PIX), BF16)],
        ),
        out_shape=[out, out],
        compiler_params=pltpu.CompilerParams(vmem_limit_bytes=40 * 2**20),
        name="finish",
    )(slots, ctile, first, order, jnp.asarray(block_rows(), BF16),
      jnp.asarray(pool_rows().T, BF16), fine, coarse, got, every, back, csum)


def plan(owner, local, c_owner, c_block, me):
    ids = np.arange(TILES)
    xs, zs, cs = ids // (NZ * NC), (ids // NC) % NZ, ids % NC
    before = jnp.asarray(ids[None, :] < ids[:, None])
    mine = lax.dynamic_slice_in_dim(owner, me * TILES, TILES)
    rank = jnp.sum((mine[:, None] == mine[None, :]) & before, axis=1)
    ox, oz, oc = mine // (NZ * NC), (mine // NC) % NZ, mine % NC
    ret_slot = jnp.where(rank == 0, mine, TILES + (oz * NX + ox) * NC + oc)
    got_slot = jnp.where(rank == 0, (oz * NC + oc) * NX + ox, TILES + (ox * NC + oc) * NZ + oz)
    hit = (owner == me).reshape(TILES, TILES)
    ordinal = jnp.sum(hit[:, None, :] & before[None], axis=2)
    local = local.reshape(TILES, TILES)
    asked, valid = [], []
    for k in range(2):
        chosen = hit & (ordinal == k)
        asked.append(jnp.sum(jnp.where(chosen, local, 0), axis=1))
        valid.append(jnp.any(chosen, axis=1))
    order_b = (ids.reshape(NX, NZ, NC).transpose(1, 0, 2)).reshape(-1)
    served = jnp.concatenate([asked[0], asked[1][order_b]])
    back_a = (ids.reshape(NX, NZ, NC).transpose(1, 2, 0)).reshape(-1)
    back_b = (ids.reshape(NX, NZ, NC).transpose(0, 2, 1)).reshape(-1)
    key = jnp.concatenate([
        jnp.where(valid[0], asked[0], TILES)[back_a],
        jnp.where(valid[1], asked[1], TILES)[back_b],
    ])
    spot = jnp.arange(SLOTS)
    place = jnp.sum((key[None, :] < key[:, None]) | ((key[None, :] == key[:, None]) & (spot[None, :] < spot[:, None])), axis=1)
    order = jnp.sum(jnp.where(place[None, :] == spot[:, None], spot[None, :], 0), axis=1)
    first = jnp.sum(key[None, :] < jnp.arange(TILES + 1)[:, None], axis=1)
    c_mine = lax.dynamic_slice_in_dim(c_owner, me * TILES, TILES)
    b_mine = lax.dynamic_slice_in_dim(c_block, me * TILES, TILES)
    ctile = ((c_mine % NC) * (NX * NZ) + c_mine // NC) * BLK + b_mine
    c_hit = spot[:, None] == ctile[None, :]
    pick_a = jnp.min(jnp.where(c_hit, ids[None, :], TILES), axis=1)
    pick_b = jnp.max(jnp.where(c_hit, ids[None, :], -1), axis=1)
    pick_b = jnp.where((pick_b == pick_a) | (pick_b < 0), TILES, pick_b)
    as_int = lambda v: v.astype(jnp.int32)
    return tuple(map(as_int, (ret_slot, got_slot, served, order, first, ctile, pick_a, pick_b)))


def body(frames, tail, cotangent, window_base, window_frac, fine_owner, fine_local, coarse_owner, coarse_block):
    frames = frames[0]
    me = lax.axis_index("space")
    ret_slot, got_slot, served, order, first, ctile, pick_a, pick_b = plan(
        fine_owner[0, :, 0], fine_local[0], coarse_owner[0, :, 0], coarse_block[0], me)
    fine, coarse, ret, terms, pooled = prep(
        ret_slot, cotangent[0], window_base[0], window_frac[0], frames, tail)
    got, back, every, csum = exchange(served, pick_a, pick_b, frames, tail, ret, terms, pooled)
    flat = lambda v: v.reshape(-1, PIX, PIX)
    grad_a, grad_b = finish(got_slot, ctile, first, order, fine, coarse, flat(got), flat(every), flat(back), csum)
    return grad_a[None], grad_b[None]


def solution(mesh):
    in_specs = (
        P("clip", "space", None, None),
        P("space", None, None),
        P("clip", "space", None, None, None),
        P("clip", "space", None, None, None),
        P("clip", "space", None, None, None),
        P("clip", None, None),
        P("clip", None),
        P("clip", None, None),
        P("clip", None),
    )
    out_specs = (P("clip", "space", None, None), P("clip", "space", None, None))
    return jax.shard_map(body, mesh=mesh, in_specs=in_specs, out_specs=out_specs, check_vma=False)
```

```python
import functools

import jax
import jax.numpy as jnp
import numpy as np
from jax import lax
from jax.experimental import pallas as pl
from jax.experimental.pallas import tpu as pltpu
from jax.sharding import PartitionSpec as P

MESH = pl.DeviceIdType.MESH
POOL = 4
SIDE = 16
WIN = 9
PIX = 256
HALF = PIX // 2
NX, NZ, NC = 4, 4, 2
BLK = 2
TILES = 32
SLOTS = 2 * TILES
F32 = jnp.float32
BF16 = jnp.bfloat16


def placement():
    spread = np.zeros((2 * WIN * SIDE, WIN * WIN), np.float32)
    for a in range(WIN):
        for k in range(WIN):
            spread[a * SIDE + k, a * WIN + k] = 1
            spread[WIN * SIDE + a * SIDE + k + 1, a * WIN + k] = 1
    return spread


def pool_rows():
    rows = np.zeros((SIDE, PIX), np.float32)
    for y in range(SIDE):
        for x in range(SIDE):
            rows[(y // POOL) * POOL + x // POOL, y * SIDE + x] = 1
    return rows


def block_rows():
    rows = np.zeros((PIX, PIX), np.float32)
    for ty in range(4):
        for tx in range(4):
            for a in range(4):
                for b in range(4):
                    rows[(ty * 4 + a) * 16 + tx * 4 + b, (ty * 4 + tx) * 16 + a * 4 + b] = 1
    return rows


def dot(a, b):
    return jnp.dot(a, b, preferred_element_type=F32)


def window_map(spread, cot, base, frac):
    placed = dot(spread, cot)
    rows = WIN * SIDE
    fx = frac[0:1].astype(F32)
    fy = frac[1:2].astype(F32)
    shape = (SIDE, PIX)
    ox = jnp.broadcast_to(base[0:1] - WIN // 2, shape)
    oy = jnp.broadcast_to(base[1:2] - WIN // 2, shape)
    across = (1.0 - fx) * placed[:rows] + fx * placed[rows:]
    groups = []
    for y in range(WIN + 1):
        value = None
        if y < WIN:
            value = (1.0 - fy) * across[y * SIDE : (y + 1) * SIDE]
        if y > 0:
            below = fy * across[(y - 1) * SIDE : y * SIDE]
            value = below if value is None else value + below
        groups.append(value)
    for step in (1, 2, 4):
        chosen = (ox & step) != 0
        groups = [jnp.where(chosen, pltpu.roll(g, step, 0), g) for g in groups]
    zero = jnp.zeros(shape, F32)
    for step in (1, 2, 4):
        chosen = (oy & step) != 0
        count = min(SIDE, len(groups) + step)
        groups = [
            jnp.where(
                chosen,
                groups[y - step] if y >= step else zero,
                groups[y] if y < len(groups) else zero,
            )
            for y in range(count)
        ]
    return jnp.concatenate(groups, axis=0).astype(BF16)


def plan_kernel(owner_ref, local_ref, c_owner_ref, c_block_ref, out_ref):
    me = lax.axis_index("space")
    total = functools.partial(jnp.sum, keepdims=True)
    sub, lane = (lax.broadcasted_iota(jnp.int32, (TILES, TILES), n) for n in range(2))
    wide_sub, wide_lane = (lax.broadcasted_iota(jnp.int32, (TILES, SLOTS), n) for n in range(2))
    tall_sub, tall_lane = (lax.broadcasted_iota(jnp.int32, (SLOTS, TILES), n) for n in range(2))
    slot_sub, slot_lane = (lax.broadcasted_iota(jnp.int32, (SLOTS, SLOTS), n) for n in range(2))
    one = (sub == lane).astype(F32)
    row_of = lambda n: lax.broadcasted_iota(jnp.int32, (TILES, 128), n)
    per_row = 128 // TILES
    pick_row = (lax.broadcasted_iota(jnp.int32, (TILES, 8), 0) // per_row == lax.broadcasted_iota(jnp.int32, (TILES, 8), 1)).astype(F32)
    in_part = row_of(0) % per_row == row_of(1) // TILES
    fold = (lax.broadcasted_iota(jnp.int32, (128, TILES), 0) % TILES == lax.broadcasted_iota(jnp.int32, (128, TILES), 1)).astype(F32)

    def square(ref):
        rows = dot(pick_row, ref[...].astype(F32))
        return dot(jnp.where(in_part, rows, 0.0), fold).astype(jnp.int32)

    owner, local, c_owner, c_block = (square(r) for r in (owner_ref, local_ref, c_owner_ref, c_block_ref))
    flip = (((0,), (0,)), ((), ()))

    def turned(v):
        return lax.dot_general(v.astype(F32), one, flip, preferred_element_type=F32).astype(jnp.int32)

    def mine(v):
        row = total(jnp.where(sub == me, v, 0), axis=0)
        return row, total(jnp.where(lane == me, turned(v), 0), axis=1)

    def parts(v):
        return v // (NZ * NC), (v // NC) % NZ, v % NC

    own_row, own_col = mine(owner)
    same = own_row == own_col
    rank_row = total(jnp.where(same & (sub < lane), 1, 0), axis=0)
    rank_col = total(jnp.where(same & (lane < sub), 1, 0), axis=1)
    ox, oz, oc = parts(own_row)
    got_slot = jnp.where(rank_row == 0, (oz * NC + oc) * NX + ox, TILES + (ox * NC + oc) * NZ + oz)
    ox, oz, oc = parts(own_col)
    ret_slot = jnp.where(rank_col == 0, own_col, TILES + (oz * NX + ox) * NC + oc)
    filled = total(jnp.where(ret_slot == wide_lane, wide_sub, 0), axis=0)

    ctile_row, ctile_col = (
        ((o % NC) * (NX * NZ) + o // NC) * BLK + b for o, b in zip(mine(c_owner), mine(c_block)))
    named = ctile_col == wide_lane
    pick_a = jnp.min(jnp.where(named, wide_sub, TILES), axis=0, keepdims=True)
    pick_b = jnp.max(jnp.where(named, wide_sub, -1), axis=0, keepdims=True)
    pick_b = jnp.where((pick_b == pick_a) | (pick_b < 0), TILES, pick_b)

    def asked(hit, ids, earlier, axis):
        seen = hit.astype(F32)
        before = dot(earlier, seen) if axis == 0 else dot(seen, earlier)
        out = []
        for k in range(2):
            chosen = hit & (before.astype(jnp.int32) == k)
            value = total(jnp.where(chosen, ids, 0), axis=axis)
            count = total(jnp.where(chosen, 1, 0), axis=axis)
            out.append((value, jnp.where(count > 0, value, TILES)))
        return out

    (_, key0_row), (_, key1_row) = asked(turned(owner) == me, turned(local), (lane < sub).astype(F32), 0)
    (ask0, key0), (ask1, key1) = asked(owner == me, local, (sub < lane).astype(F32), 1)
    px, pz, pc = parts(wide_sub)
    served = total(jnp.where(wide_lane == wide_sub, ask0, 0), axis=0)
    served += total(jnp.where(wide_lane == TILES + (pz * NX + px) * NC + pc, ask1, 0), axis=0)
    key_row = total(jnp.where(wide_lane == (pz * NC + pc) * NX + px, key0, 0), axis=0)
    key_row += total(jnp.where(wide_lane == TILES + (px * NC + pc) * NZ + pz, key1, 0), axis=0)
    px, pz, pc = parts(tall_lane)
    key_col = total(jnp.where(tall_sub == (pz * NC + pc) * NX + px, key0_row, 0), axis=1)
    key_col += total(jnp.where(tall_sub == TILES + (px * NC + pc) * NZ + pz, key1_row, 0), axis=1)
    ahead = (key_row < key_col) | ((key_row == key_col) & (slot_lane < slot_sub))
    place = total(jnp.where(ahead, 1, 0), axis=1)
    order = total(jnp.where(place == slot_lane, slot_sub, 0), axis=0)
    first = total(jnp.where(key_col < slot_lane, 1, 0), axis=0)
    out_ref[...] = jnp.zeros((8, SLOTS), jnp.int32)
    for row, value in enumerate((served, filled, pick_a, pick_b, ctile_row, got_slot, order, first)):
        out_ref[row : row + 1, : value.shape[1]] = value


SERVED, FILLED, PICK_A, PICK_B, CTILE, GOT, ORDER, FIRST = range(8)


def plan(*ids):
    vmem = pl.BlockSpec(memory_space=pltpu.VMEM)
    return pl.pallas_call(
        plan_kernel, in_specs=[vmem] * 4, out_specs=vmem,
        out_shape=jax.ShapeDtypeStruct((8, SLOTS), jnp.int32), name="plan",
    )(*ids)


def exchange_kernel(
    table, spread_ref, pool_ref, perm_ref, widen_ref, base, frac, frames, tail, cot_ref,
    got, grad_ref, maps_ref, query_ref, back, below_every, every, ret_a, ret_b, get_a, get_b,
    first, cot, tiles, fine, other, terms, slots, partial, sibling, raw, pown,
    up_a, down_a, up_b, down_b, red_a, red_b, mid_a, mid_b, last_a, last_b, coarse, running,
    send, recv, local
):
    scale = 1.0 / 16.0
    clip = lax.axis_index("clip")
    space = lax.axis_index("space")
    x = space // (NZ * NC)
    z = (space // NC) % NZ
    c = space % NC
    counts = {"remote": 0, "local": 0}

    def along_x(d, core=0):
        return (clip, (((x + d) % NX) * NZ + z) * NC + (c + core) % NC)

    def along_z(d, core=0):
        return (clip, (x * NZ + (z + d) % NZ) * NC + (c + core) % NC)

    def remote(src, dst, device):
        n = counts["remote"]
        counts["remote"] += 1
        return pltpu.make_async_remote_copy(
            src_ref=src, dst_ref=dst, send_sem=send.at[n], recv_sem=recv.at[n],
            device_id=device, device_id_type=MESH)

    def here(src, dst):
        n = counts["local"]
        counts["local"] += 1
        return pltpu.make_async_copy(src, dst, local.at[n])

    def start(copies):
        for copy in copies:
            copy.start()
        return copies

    def arrive(copies):
        for copy in copies:
            copy.wait_recv()

    load = start([here(frames, first.at[pl.ds(0, TILES)]), here(cot_ref, cot)])
    at_end = clip == 3
    below = ((clip + 3) % 4, space)
    move_tiles = remote(frames, tiles, below)
    end_tiles = here(tail, tiles)
    pool_tail = here(tail, slots.at[pl.ds(0, TILES)])

    @pl.when(at_end)
    def _():
        end_tiles.start()

    @pl.when(clip == 0)
    def _():
        pool_tail.start()

    barrier = pltpu.get_barrier_semaphore()
    greeted = [along_x(d, k) for d in range(1, NX) for k in range(NC)]
    greeted += [along_z(d, k) for d in range(1, NZ) for k in range(NC)]
    greeted += [along_x(0, 1), ((clip + 1) % 4, space)]
    for device in greeted:
        pl.semaphore_signal(barrier, inc=1, device_id=device, device_id_type=MESH)
    pl.semaphore_wait(barrier, len(greeted))

    sent = []

    def pool(source, target):
        def one(n, carry):
            rows = pl.ds(pl.multiple_of((n % 16) * SIDE, SIDE), SIDE)
            raw[n // 16, rows, :] = (dot(pool_ref[...], source[n]) * scale).astype(BF16)
            return carry
        lax.fori_loop(0, TILES, one, 0)
        for b in range(BLK):
            target[b] = dot(perm_ref[...], raw[b]).astype(BF16)

    @pl.when(clip > 0)
    def _():
        move_tiles.start()

    load[0].wait()

    @pl.when(clip > 0)
    def _():
        pool(first, pown)

    @pl.when(clip == 0)
    def _():
        pool_tail.wait()
        pool(slots, pown)

    top, bottom = pl.ds(0, HALF), pl.ds(HALF, HALF)
    keep_pool = start([here(pown, every.at[c, x, z])])
    pool_a1 = start([remote(pown.at[:, top], every.at[c, x, z, :, top], along_x(d)) for d in range(1, NX)])
    pool_b1 = start([remote(pown.at[:, bottom], every.at[c, x, z, :, bottom], along_z(d)) for d in range(1, NZ)])
    sent += pool_a1 + pool_b1

    def products(begin, end, level, keep, put):
        def one(n, carry):
            for q in (2 * n, 2 * n + 1):
                weights = window_map(spread_ref[...], cot[q, level], base[q, level], frac[q, level])
                put[q] = (dot(weights, first[q]) * scale).astype(BF16)
                keep[q] = weights.T
            return carry
        lax.fori_loop(begin // 2, end // 2, one, 0)

    load[1].wait()
    products(0, TILES // 2, 0, fine, terms)

    keep_pool[0].wait()
    arrive(pool_a1)
    line = every.at[c, :, z, :, top]
    pool_a2 = start([remote(line, line, along_z(d)) for d in (1, NZ - 1)])
    arrive(pool_b1)
    line = every.at[c, x, :, :, bottom]
    pool_b2 = start([remote(line, line, along_x(d)) for d in (1, NX - 1)])
    sent += pool_a2 + pool_b2

    products(TILES // 2, TILES, 0, fine, terms)
    put_maps = start([here(fine, maps_ref)])

    def fill_slots(half, source, row):
        def one(n, carry):
            slots[half * TILES + n] = source[table[row, half * TILES + n]]
            return carry
        lax.fori_loop(0, TILES, one, 0)

    def group(half, n):
        return slots.at[pl.ds(half * TILES + n * 8, 8)]

    def first_hop(source, row, into_a, into_b):
        fill_slots(0, source, row)
        stay_a = start([here(group(0, x), into_a.at[:, x])])
        hop_a = start([remote(group(0, (x + d) % NX), into_a.at[:, x], along_x(d)) for d in range(1, NX)])
        fill_slots(1, source, row)
        stay_b = start([here(group(1, z), into_b.at[:, z])])
        hop_b = start([remote(group(1, (z + d) % NZ), into_b.at[:, z], along_z(d)) for d in range(1, NZ)])
        return stay_a, hop_a, stay_b, hop_b

    others = [(d, k) for d in range(NZ) for k in range(NC) if d or k]

    def second_hop(hops, from_a, from_b, into):
        stay_a, hop_a, stay_b, hop_b = hops
        into_a = into.at[pl.ds((z * NC + c) * 4, 4)]
        into_b = into.at[pl.ds(TILES + (x * NC + c) * 4, 4)]
        stay_a[0].wait()
        arrive(hop_a)
        far = start([remote(from_a.at[(z + d) % NZ * NC + (c + k) % NC], into_a, along_z(d, k)) for d, k in others])
        near = start([here(from_a.at[z * NC + c], into_a)])
        stay_b[0].wait()
        arrive(hop_b)
        far += start([remote(from_b.at[(x + d) % NX * NC + (c + k) % NC], into_b, along_x(d, k)) for d, k in others])
        near += start([here(from_b.at[x * NC + c], into_b)])
        return far, near

    ret_hops = first_hop(terms, FILLED, ret_a, ret_b)

    products(0, TILES // 2, 1, other, first)

    x_up, x_down, z_up, z_down = (x + 1) % NX, (x + NX - 1) % NX, (z + 1) % NZ, (z + NZ - 1) % NZ
    low, high = pl.ds(0, 2), pl.ds(2, 2)
    arrive(pool_a2)
    line_up, line_down = every.at[c, low, z_down, :, top], every.at[c, high, z_up, :, top]
    pool_a3 = start([remote(line_up, line_up, along_z(1)), remote(line_down, line_down, along_z(NZ - 1))])
    arrive(pool_b2)
    line_up, line_down = every.at[c, x_down, low, :, bottom], every.at[c, x_up, high, :, bottom]
    pool_b3 = start([remote(line_up, line_up, along_x(1)), remote(line_down, line_down, along_x(NX - 1))])
    sent += pool_a3 + pool_b3

    products(TILES // 2, TILES, 1, other, first)
    first[TILES] = jnp.zeros((PIX, PIX), BF16)

    def fill(which, core):
        def one(n, carry):
            value = first[table[PICK_A, core * TILES + n]].astype(F32)
            value = value + first[table[PICK_B, core * TILES + n]].astype(F32)
            partial[which, n // (NZ * BLK), (n // BLK) % NZ, n % BLK] = value.astype(BF16)
            return carry
        lax.fori_loop(0, TILES, one, 0)

    fill(1, 1 - c)
    share = start([remote(partial.at[1], sibling, along_x(0, 1))])
    fill(0, c)
    arrive(share)

    def join(n, carry):
        at = (n // (NZ * BLK), (n // BLK) % NZ, n % BLK)
        mine = partial[(0, *at)].astype(F32)
        partial[(0, *at)] = (mine + sibling[at].astype(F32)).astype(BF16)
        return carry

    lax.fori_loop(0, TILES, join, 0)

    mine = partial.at[0]
    z_far, x_far = (z + 2) % NZ, (x + 2) % NX
    red_1 = start([
        remote(mine.at[low, z_far, :, top], up_a, along_z(1)),
        remote(mine.at[high, z_far, :, top], down_a, along_z(NZ - 1)),
        remote(mine.at[x_far, low, :, bottom], up_b, along_x(1)),
        remote(mine.at[x_far, high, :, bottom], down_b, along_x(NX - 1)),
    ])
    arrive(red_1)

    def pass_on(n, carry):
        i, b = n // BLK, n % BLK
        for at, extra in (
            ((0, i, z_up, b, top), up_a), ((0, i + 2, z_down, b, top), down_a),
            ((0, x_up, i, b, bottom), up_b), ((0, x_down, i + 2, b, bottom), down_b),
        ):
            partial[at] = (partial[at].astype(F32) + extra[i, b].astype(F32)).astype(BF16)
        return carry

    lax.fori_loop(0, 2 * BLK, pass_on, 0)
    red_2 = start([
        remote(mine.at[:, z_up, :, top], red_a.at[0], along_z(1)),
        remote(mine.at[:, z_down, :, top], red_a.at[1], along_z(NZ - 1)),
        remote(mine.at[x_up, :, :, bottom], red_b.at[0], along_x(1)),
        remote(mine.at[x_down, :, :, bottom], red_b.at[1], along_x(NX - 1)),
    ])

    ret_far, stay = second_hop(ret_hops, ret_a, ret_b, back)
    sent += ret_far

    arrive(red_2)

    def middle(n, carry):
        i, b = n // BLK, n % BLK
        for at, extra, into in (((0, i, z, b, top), red_a, mid_a), ((0, x, i, b, bottom), red_b, mid_b)):
            value = partial[at].astype(F32) + extra[0, i, b].astype(F32) + extra[1, i, b].astype(F32)
            into[i, b] = value.astype(BF16)
        return carry

    lax.fori_loop(0, NX * BLK, middle, 0)
    red_a2 = start([remote(mid_a.at[(x + d) % NX], last_a.at[x], along_x(d)) for d in range(1, NX)])
    red_b2 = start([remote(mid_b.at[(z + d) % NZ], last_b.at[z], along_z(d)) for d in range(1, NZ)])
    sent += red_a2 + red_b2
    last_a[x] = mid_a[x]
    last_b[z] = mid_b[z]

    for copy in ret_hops[1] + ret_hops[3]:
        copy.wait_send()

    @pl.when(at_end)
    def _():
        end_tiles.wait()

    @pl.when(clip < 3)
    def _():
        move_tiles.wait_recv()

    get_hops = first_hop(tiles, SERVED, get_a, get_b)

    arrive(pool_a3)
    arrive(pool_b3)
    pool_4 = start([remote(every.at[c], below_every.at[c], below)])

    def total(buffer, at):
        value = buffer[(0, *at)].astype(F32)
        for n in range(1, 4):
            value = value + buffer[(n, *at)].astype(F32)
        return value

    arrive(red_a2)
    arrive(red_b2)
    for b in range(BLK):
        coarse[b, top] = total(last_a, (b,)).astype(BF16)
        coarse[b, bottom] = total(last_b, (b,)).astype(BF16)
    flip = (((0,), (0,)), ((), ()))
    for b in range(BLK):
        raw[b] = lax.dot_general(perm_ref[...], coarse[b], flip, preferred_element_type=F32).astype(BF16)

    get_far, near = second_hop(get_hops, get_a, get_b, got)
    sent += get_far
    stay += near

    arrive(pool_4)
    pool_5 = start([remote(below_every.at[c], below_every.at[c], along_x(0, 1))])
    sent += pool_4 + pool_5

    arrive(ret_far)
    for copy in get_hops[1] + get_hops[3]:
        copy.wait_send()
    for copy in stay:
        copy.wait()
    load_back = start([here(back, slots)])
    load_back[0].wait()
    for part in range(4):
        rows = pl.ds(part * 64, 64)
        running[0] = jnp.zeros((64, PIX), F32)

        def add(n, carry):
            running[n + 1] = running[n] + slots[table[ORDER, n], rows].astype(F32)
            return carry

        lax.fori_loop(0, SLOTS, add, 0)

        def gradient(n, carry):
            at = pl.ds(pl.multiple_of((n % 16) * SIDE, SIDE), SIDE)
            value = dot(widen_ref[rows], raw[n // 16, at]) * scale
            value = value + (running[table[FIRST, n + 1]] - running[table[FIRST, n]])
            terms[n, rows] = value.astype(BF16)
            return carry

        lax.fori_loop(0, TILES, gradient, 0)
    put = start([here(terms, grad_ref)])

    for copy in share + red_1 + red_2:
        copy.wait_send()
    arrive(pool_5)
    load_every = start([here(below_every, partial)])
    load_every[0].wait()

    def query(n, carry):
        at = table[CTILE, n]
        tile = partial[at // (NX * NZ * BLK), (at // (NZ * BLK)) % NX, (at // BLK) % NZ, at % BLK]
        other[n] = (dot(other[n], tile) * scale).astype(BF16)
        return carry

    lax.fori_loop(0, TILES, query, 0)
    put += start([here(other, query_ref)])

    arrive(get_far)
    for copy in put + put_maps:
        copy.wait()
    for copy in sent:
        copy.wait_send()

    @pl.when(clip > 0)
    def _():
        move_tiles.wait_send()


def exchange(table, frames, tail, cot, base, frac):
    smem = pl.BlockSpec(memory_space=pltpu.SMEM)
    vmem = pl.BlockSpec(memory_space=pltpu.VMEM)
    hbm = pl.BlockSpec(memory_space=pl.ANY)
    tile = (PIX, PIX)
    shape = lambda *s: jax.ShapeDtypeStruct(s + tile, BF16)
    half = lambda *s: pltpu.VMEM(s + (HALF, PIX), BF16)
    full = lambda *s: pltpu.VMEM(s + tile, BF16)
    outs = pl.pallas_call(
        exchange_kernel,
        in_specs=[smem] + [vmem] * 6 + [hbm] * 3,
        out_specs=[hbm] * 11,
        out_shape=[
            shape(SLOTS), shape(TILES), shape(TILES), shape(TILES), shape(SLOTS),
            shape(NC, NX, NZ, BLK), shape(NC, NX, NZ, BLK),
            shape(8, NX), shape(8, NZ), shape(8, NX), shape(8, NZ),
        ],
        scratch_shapes=[
            full(TILES + 1), pltpu.VMEM((TILES, 2, WIN * WIN, PIX), BF16),
            full(TILES), full(TILES), full(TILES), full(TILES),
            full(SLOTS), full(2, NX, NZ, BLK), full(NX, NZ, BLK),
            full(BLK), full(BLK),
            half(2, BLK), half(2, BLK), half(2, BLK), half(2, BLK),
            half(2, NX, BLK), half(2, NZ, BLK), half(NX, BLK), half(NZ, BLK),
            half(NX, BLK), half(NZ, BLK), full(BLK), pltpu.VMEM((SLOTS + 1, 64, PIX), F32),
            pltpu.SemaphoreType.DMA((80,)), pltpu.SemaphoreType.DMA((80,)),
            pltpu.SemaphoreType.DMA((24,)),
        ],
        compiler_params=pltpu.CompilerParams(
            collective_id=0, has_side_effects=True, vmem_limit_bytes=62 * 2**20),
        name="exchange",
    )(table, jnp.asarray(placement(), BF16), jnp.asarray(pool_rows(), BF16),
      jnp.asarray(block_rows(), BF16), jnp.asarray(pool_rows().T, BF16), base, frac, frames, tail, cot)
    return outs[:4]


GROUP = 4


def finish_kernel(table, maps_ref, query_ref, *refs):
    for n in range(GROUP):
        value = dot(maps_ref[n], refs[n][0]) * (1.0 / 16.0)
        refs[GROUP][n] = (value + query_ref[n].astype(F32)).astype(BF16)


def finish(table, maps, query, got):
    tile = lambda q, t: (q, 0, 0)
    block = pl.BlockSpec((GROUP, PIX, PIX), tile)
    return pl.pallas_call(
        finish_kernel,
        grid_spec=pltpu.PrefetchScalarGridSpec(
            num_scalar_prefetch=1,
            grid=(TILES // GROUP,),
            in_specs=[block, block] + [
                pl.BlockSpec((1, PIX, PIX), lambda q, t, n=n: (t[GOT, q * GROUP + n], 0, 0))
                for n in range(GROUP)
            ],
            out_specs=block,
        ),
        out_shape=jax.ShapeDtypeStruct((TILES, PIX, PIX), BF16),
        compiler_params=pltpu.CompilerParams(vmem_limit_bytes=60 * 2**20),
        name="finish",
    )(table, maps, query, *[got] * GROUP)


def body(frames, tail, cotangent, window_base, window_frac, fine_owner, fine_local, coarse_owner, coarse_block):
    table = plan(*(v.reshape(8, 128) for v in (fine_owner, fine_local, coarse_owner, coarse_block)))
    got, grad_b, maps, query = exchange(table, frames[0], tail, cotangent[0], window_base[0], window_frac[0])
    grad_a = finish(table, maps, query, got)
    return grad_a[None], grad_b[None]


def solution(mesh):
    in_specs = (
        P("clip", "space", None, None),
        P("space", None, None),
        P("clip", "space", None, None, None),
        P("clip", "space", None, None, None),
        P("clip", "space", None, None, None),
        P("clip", None, None),
        P("clip", None),
        P("clip", None, None),
        P("clip", None),
    )
    out_specs = (P("clip", "space", None, None), P("clip", "space", None, None))
    return jax.shard_map(body, mesh=mesh, in_specs=in_specs, out_specs=out_specs, check_vma=False)
```

```python
import functools

import jax
import jax.numpy as jnp
import numpy as np
from jax import lax
from jax.experimental import pallas as pl
from jax.experimental.pallas import tpu as pltpu
from jax.sharding import PartitionSpec as P

MESH = pl.DeviceIdType.MESH
POOL = 4
SIDE = 16
WIN = 9
PIX = 256
HALF = PIX // 2
NX, NZ, NC = 4, 4, 2
BLK = 2
TILES = 32
SLOTS = 2 * TILES
F32 = jnp.float32
BF16 = jnp.bfloat16


def placement():
    spread = np.zeros((2 * WIN * SIDE, WIN * WIN), np.float32)
    for a in range(WIN):
        for k in range(WIN):
            spread[a * SIDE + k, a * WIN + k] = 1
            spread[WIN * SIDE + a * SIDE + k + 1, a * WIN + k] = 1
    return spread


def pool_rows():
    rows = np.zeros((SIDE, PIX), np.float32)
    for y in range(SIDE):
        for x in range(SIDE):
            rows[(y // POOL) * POOL + x // POOL, y * SIDE + x] = 1
    return rows


def block_rows():
    rows = np.zeros((PIX, PIX), np.float32)
    for ty in range(4):
        for tx in range(4):
            for a in range(4):
                for b in range(4):
                    rows[(ty * 4 + a) * 16 + tx * 4 + b, (ty * 4 + tx) * 16 + a * 4 + b] = 1
    return rows


def dot(a, b):
    return jnp.dot(a, b, preferred_element_type=F32)


def window_map(spread, cot, base, frac):
    placed = dot(spread, cot)
    rows = WIN * SIDE
    fx = frac[0:1].astype(F32)
    fy = frac[1:2].astype(F32)
    shape = (SIDE, PIX)
    ox = jnp.broadcast_to(base[0:1] - WIN // 2, shape)
    oy = jnp.broadcast_to(base[1:2] - WIN // 2, shape)
    across = (1.0 - fx) * placed[:rows] + fx * placed[rows:]
    groups = []
    for y in range(WIN + 1):
        value = None
        if y < WIN:
            value = (1.0 - fy) * across[y * SIDE : (y + 1) * SIDE]
        if y > 0:
            below = fy * across[(y - 1) * SIDE : y * SIDE]
            value = below if value is None else value + below
        groups.append(value)
    for step in (1, 2, 4):
        chosen = (ox & step) != 0
        groups = [jnp.where(chosen, pltpu.roll(g, step, 0), g) for g in groups]
    zero = jnp.zeros(shape, F32)
    for step in (1, 2, 4):
        chosen = (oy & step) != 0
        count = min(SIDE, len(groups) + step)
        groups = [
            jnp.where(
                chosen,
                groups[y - step] if y >= step else zero,
                groups[y] if y < len(groups) else zero,
            )
            for y in range(count)
        ]
    return jnp.concatenate(groups, axis=0).astype(BF16)


def plan_kernel(owner_ref, local_ref, c_owner_ref, c_block_ref, out_ref):
    me = lax.axis_index("space")
    total = functools.partial(jnp.sum, keepdims=True)
    sub, lane = (lax.broadcasted_iota(jnp.int32, (TILES, TILES), n) for n in range(2))
    wide_sub, wide_lane = (lax.broadcasted_iota(jnp.int32, (TILES, SLOTS), n) for n in range(2))
    tall_sub, tall_lane = (lax.broadcasted_iota(jnp.int32, (SLOTS, TILES), n) for n in range(2))
    slot_sub, slot_lane = (lax.broadcasted_iota(jnp.int32, (SLOTS, SLOTS), n) for n in range(2))
    one = (sub == lane).astype(F32)
    row_of = lambda n: lax.broadcasted_iota(jnp.int32, (TILES, 128), n)
    per_row = 128 // TILES
    pick_row = (lax.broadcasted_iota(jnp.int32, (TILES, 8), 0) // per_row == lax.broadcasted_iota(jnp.int32, (TILES, 8), 1)).astype(F32)
    in_part = row_of(0) % per_row == row_of(1) // TILES
    fold = (lax.broadcasted_iota(jnp.int32, (128, TILES), 0) % TILES == lax.broadcasted_iota(jnp.int32, (128, TILES), 1)).astype(F32)

    def square(ref):
        rows = dot(pick_row, ref[...].astype(F32))
        return dot(jnp.where(in_part, rows, 0.0), fold).astype(jnp.int32)

    owner, local, c_owner, c_block = (square(r) for r in (owner_ref, local_ref, c_owner_ref, c_block_ref))
    flip = (((0,), (0,)), ((), ()))

    def turned(v):
        return lax.dot_general(v.astype(F32), one, flip, preferred_element_type=F32).astype(jnp.int32)

    def mine(v):
        row = total(jnp.where(sub == me, v, 0), axis=0)
        return row, total(jnp.where(lane == me, turned(v), 0), axis=1)

    def parts(v):
        return v // (NZ * NC), (v // NC) % NZ, v % NC

    own_row, own_col = mine(owner)
    same = own_row == own_col
    rank_row = total(jnp.where(same & (sub < lane), 1, 0), axis=0)
    rank_col = total(jnp.where(same & (lane < sub), 1, 0), axis=1)
    ox, oz, oc = parts(own_row)
    got_slot = jnp.where(rank_row == 0, (oz * NC + oc) * NX + ox, TILES + (ox * NC + oc) * NZ + oz)
    ox, oz, oc = parts(own_col)
    ret_slot = jnp.where(rank_col == 0, own_col, TILES + (oz * NX + ox) * NC + oc)
    filled = total(jnp.where(ret_slot == wide_lane, wide_sub, 0), axis=0)

    ctile_row, ctile_col = (
        ((o % NC) * (NX * NZ) + o // NC) * BLK + b for o, b in zip(mine(c_owner), mine(c_block)))
    named = ctile_col == wide_lane
    pick_a = jnp.min(jnp.where(named, wide_sub, TILES), axis=0, keepdims=True)
    pick_b = jnp.max(jnp.where(named, wide_sub, -1), axis=0, keepdims=True)
    pick_b = jnp.where((pick_b == pick_a) | (pick_b < 0), TILES, pick_b)

    def asked(hit, ids, earlier, axis):
        seen = hit.astype(F32)
        before = dot(earlier, seen) if axis == 0 else dot(seen, earlier)
        out = []
        for k in range(2):
            chosen = hit & (before.astype(jnp.int32) == k)
            value = total(jnp.where(chosen, ids, 0), axis=axis)
            count = total(jnp.where(chosen, 1, 0), axis=axis)
            out.append((value, jnp.where(count > 0, value, TILES)))
        return out

    (_, key0_row), (_, key1_row) = asked(turned(owner) == me, turned(local), (lane < sub).astype(F32), 0)
    (ask0, key0), (ask1, key1) = asked(owner == me, local, (sub < lane).astype(F32), 1)
    px, pz, pc = parts(wide_sub)
    served = total(jnp.where(wide_lane == wide_sub, ask0, 0), axis=0)
    served += total(jnp.where(wide_lane == TILES + (pz * NX + px) * NC + pc, ask1, 0), axis=0)
    key_row = total(jnp.where(wide_lane == (pz * NC + pc) * NX + px, key0, 0), axis=0)
    key_row += total(jnp.where(wide_lane == TILES + (px * NC + pc) * NZ + pz, key1, 0), axis=0)
    px, pz, pc = parts(tall_lane)
    key_col = total(jnp.where(tall_sub == (pz * NC + pc) * NX + px, key0_row, 0), axis=1)
    key_col += total(jnp.where(tall_sub == TILES + (px * NC + pc) * NZ + pz, key1_row, 0), axis=1)
    ahead = (key_row < key_col) | ((key_row == key_col) & (slot_lane < slot_sub))
    place = total(jnp.where(ahead, 1, 0), axis=1)
    order = total(jnp.where(place == slot_lane, slot_sub, 0), axis=0)
    first = total(jnp.where(key_col < slot_lane, 1, 0), axis=0)
    out_ref[...] = jnp.zeros((8, SLOTS), jnp.int32)
    for row, value in enumerate((served, filled, pick_a, pick_b, ctile_row, got_slot, order, first)):
        out_ref[row : row + 1, : value.shape[1]] = value


SERVED, FILLED, PICK_A, PICK_B, CTILE, GOT, ORDER, FIRST = range(8)


def plan(*ids):
    vmem = pl.BlockSpec(memory_space=pltpu.VMEM)
    return pl.pallas_call(
        plan_kernel, in_specs=[vmem] * 4, out_specs=vmem,
        out_shape=jax.ShapeDtypeStruct((8, SLOTS), jnp.int32), name="plan",
    )(*ids)


def exchange_kernel(
    table, spread_ref, pool_ref, perm_ref, widen_ref, base, frac, frames, tail, cot_ref,
    fine, terms, back, every, ret_a, ret_b, get_a, get_b,
    first, cot, tiles, other, got, slots, partial, sibling, raw, pown, pbuf,
    up_a, down_a, up_b, down_b, red_a, red_b, mid_a, mid_b, last_a, last_b, coarse, running,
    send, recv, local
):
    scale = 1.0 / 16.0
    clip = lax.axis_index("clip")
    space = lax.axis_index("space")
    x = space // (NZ * NC)
    z = (space // NC) % NZ
    c = space % NC
    counts = {"remote": 0, "local": 0}

    def along_x(d, core=0):
        return (clip, (((x + d) % NX) * NZ + z) * NC + (c + core) % NC)

    def along_z(d, core=0):
        return (clip, (x * NZ + (z + d) % NZ) * NC + (c + core) % NC)

    def remote(src, dst, device):
        n = counts["remote"]
        counts["remote"] += 1
        return pltpu.make_async_remote_copy(
            src_ref=src, dst_ref=dst, send_sem=send.at[n], recv_sem=recv.at[n],
            device_id=device, device_id_type=MESH)

    def here(src, dst):
        n = counts["local"]
        counts["local"] += 1
        return pltpu.make_async_copy(src, dst, local.at[n])

    def start(copies):
        for copy in copies:
            copy.start()
        return copies

    def arrive(copies):
        for copy in copies:
            copy.wait_recv()

    load = start([here(frames, first.at[pl.ds(0, TILES)]), here(cot_ref, cot)])
    at_end = clip == 3
    below = ((clip + 3) % 4, space)
    move_tiles = remote(frames, tiles, below)
    end_tiles = here(tail, tiles)
    move_pool = remote(pown, pbuf, below)

    @pl.when(at_end)
    def _():
        end_tiles.start()

    barrier = pltpu.get_barrier_semaphore()
    greeted = [along_x(d, k) for d in range(1, NX) for k in range(NC)]
    greeted += [along_z(d, k) for d in range(1, NZ) for k in range(NC)]
    greeted += [along_x(0, 1), ((clip + 1) % 4, space)]
    for device in greeted:
        pl.semaphore_signal(barrier, inc=1, device_id=device, device_id_type=MESH)
    pl.semaphore_wait(barrier, len(greeted))

    sent = []

    def pool(source, target):
        def one(n, carry):
            rows = pl.ds(pl.multiple_of((n % 16) * SIDE, SIDE), SIDE)
            raw[n // 16, rows, :] = (dot(pool_ref[...], source[n]) * scale).astype(BF16)
            return carry
        lax.fori_loop(0, TILES, one, 0)
        for b in range(BLK):
            target[b] = dot(perm_ref[...], raw[b]).astype(BF16)

    def products(begin, end, level, keep, put):
        def one(n, carry):
            for q in (2 * n, 2 * n + 1):
                weights = window_map(spread_ref[...], cot[q, level], base[q, level], frac[q, level])
                put[q] = (dot(weights, first[q]) * scale).astype(BF16)
                keep[q] = weights.T
            return carry
        lax.fori_loop(begin // 2, end // 2, one, 0)

    load[0].wait()
    pool(first, pown)

    @pl.when(clip > 0)
    def _():
        move_pool.start()
        move_tiles.start()

    @pl.when(at_end)
    def _():
        end_tiles.wait()
        pool(tiles, pbuf)

    load[1].wait()
    products(0, TILES // 4, 0, fine, terms)

    @pl.when(clip < 3)
    def _():
        move_pool.wait_recv()

    top, bottom = pl.ds(0, HALF), pl.ds(HALF, HALF)
    keep_pool = start([here(pbuf, every.at[c, x, z])])
    pool_a1 = start([remote(pbuf.at[:, top], every.at[c, x, z, :, top], along_x(d)) for d in (2, 1, 3)])
    pool_b1 = start([remote(pbuf.at[:, bottom], every.at[c, x, z, :, bottom], along_z(d)) for d in (2, 1, 3)])
    sent += pool_a1 + pool_b1

    products(TILES // 4, TILES // 2, 0, fine, terms)

    keep_pool[0].wait()
    arrive(pool_a1)
    line = every.at[c, :, z, :, top]
    pool_a2 = start([remote(line, line, along_z(d)) for d in (1, NZ - 1)])
    arrive(pool_b1)
    line = every.at[c, x, :, :, bottom]
    pool_b2 = start([remote(line, line, along_x(d)) for d in (1, NX - 1)])
    sent += pool_a2 + pool_b2

    products(TILES // 2, TILES, 0, fine, terms)

    def fill_slots(half, source, row):
        def one(n, carry):
            slots[half * TILES + n] = source[table[row, half * TILES + n]]
            return carry
        lax.fori_loop(0, TILES, one, 0)

    def group(half, n):
        return slots.at[pl.ds(half * TILES + n * 8, 8)]

    def first_hop(source, row, into_a, into_b):
        fill_slots(0, source, row)
        stay_a = start([here(group(0, x), into_a.at[:, x])])
        hop_a = start([remote(group(0, (x + d) % NX), into_a.at[:, x], along_x(d)) for d in (2, 1, 3)])
        fill_slots(1, source, row)
        stay_b = start([here(group(1, z), into_b.at[:, z])])
        hop_b = start([remote(group(1, (z + d) % NZ), into_b.at[:, z], along_z(d)) for d in (2, 1, 3)])
        return stay_a, hop_a, stay_b, hop_b

    others = [(2, 0), (2, 1), (1, 0), (3, 0), (1, 1), (3, 1), (0, 1)]

    def second_hop(hops, from_a, from_b, into):
        stay_a, hop_a, stay_b, hop_b = hops
        into_a = into.at[pl.ds((z * NC + c) * 4, 4)]
        into_b = into.at[pl.ds(TILES + (x * NC + c) * 4, 4)]
        stay_a[0].wait()
        arrive(hop_a)
        far = start([remote(from_a.at[(z + d) % NZ * NC + (c + k) % NC], into_a, along_z(d, k)) for d, k in others])
        near = start([here(from_a.at[z * NC + c], into_a)])
        stay_b[0].wait()
        arrive(hop_b)
        far += start([remote(from_b.at[(x + d) % NX * NC + (c + k) % NC], into_b, along_x(d, k)) for d, k in others])
        near += start([here(from_b.at[x * NC + c], into_b)])
        return far, near

    ret_hops = first_hop(terms, FILLED, ret_a, ret_b)

    products(0, TILES // 2, 1, other, first)

    x_up, x_down, z_up, z_down = (x + 1) % NX, (x + NX - 1) % NX, (z + 1) % NZ, (z + NZ - 1) % NZ
    low, high = pl.ds(0, 2), pl.ds(2, 2)
    arrive(pool_a2)
    line_up, line_down = every.at[c, low, z_down, :, top], every.at[c, high, z_up, :, top]
    pool_a3 = start([remote(line_up, line_up, along_z(1)), remote(line_down, line_down, along_z(NZ - 1))])
    arrive(pool_b2)
    line_up, line_down = every.at[c, x_down, low, :, bottom], every.at[c, x_up, high, :, bottom]
    pool_b3 = start([remote(line_up, line_up, along_x(1)), remote(line_down, line_down, along_x(NX - 1))])
    sent += pool_a3 + pool_b3

    products(TILES // 2, TILES, 1, other, first)
    first[TILES] = jnp.zeros((PIX, PIX), BF16)

    def fill(which, core):
        def one(n, carry):
            value = first[table[PICK_A, core * TILES + n]].astype(F32)
            value = value + first[table[PICK_B, core * TILES + n]].astype(F32)
            partial[which, n // (NZ * BLK), (n // BLK) % NZ, n % BLK] = value.astype(BF16)
            return carry
        lax.fori_loop(0, TILES, one, 0)

    fill(1, 1 - c)
    share = start([remote(partial.at[1], sibling, along_x(0, 1))])
    fill(0, c)
    arrive(share)

    def join(n, carry):
        at = (n // (NZ * BLK), (n // BLK) % NZ, n % BLK)
        mine = partial[(0, *at)].astype(F32)
        partial[(0, *at)] = (mine + sibling[at].astype(F32)).astype(BF16)
        return carry

    lax.fori_loop(0, TILES, join, 0)

    mine = partial.at[0]
    z_far, x_far = (z + 2) % NZ, (x + 2) % NX
    red_1 = start([
        remote(mine.at[low, z_far, :, top], up_a, along_z(1)),
        remote(mine.at[high, z_far, :, top], down_a, along_z(NZ - 1)),
        remote(mine.at[x_far, low, :, bottom], up_b, along_x(1)),
        remote(mine.at[x_far, high, :, bottom], down_b, along_x(NX - 1)),
    ])
    arrive(red_1)

    def pass_on(n, carry):
        i, b = n // BLK, n % BLK
        for at, extra in (
            ((0, i, z_up, b, top), up_a), ((0, i + 2, z_down, b, top), down_a),
            ((0, x_up, i, b, bottom), up_b), ((0, x_down, i + 2, b, bottom), down_b),
        ):
            partial[at] = (partial[at].astype(F32) + extra[i, b].astype(F32)).astype(BF16)
        return carry

    lax.fori_loop(0, 2 * BLK, pass_on, 0)
    red_2 = start([
        remote(mine.at[:, z_up, :, top], red_a.at[0], along_z(1)),
        remote(mine.at[:, z_down, :, top], red_a.at[1], along_z(NZ - 1)),
        remote(mine.at[x_up, :, :, bottom], red_b.at[0], along_x(1)),
        remote(mine.at[x_down, :, :, bottom], red_b.at[1], along_x(NX - 1)),
    ])

    ret_far, stay = second_hop(ret_hops, ret_a, ret_b, back)
    sent += ret_far

    arrive(red_2)

    def middle(n, carry):
        i, b = n // BLK, n % BLK
        for at, extra, into in (((0, i, z, b, top), red_a, mid_a), ((0, x, i, b, bottom), red_b, mid_b)):
            value = partial[at].astype(F32) + extra[0, i, b].astype(F32) + extra[1, i, b].astype(F32)
            into[i, b] = value.astype(BF16)
        return carry

    lax.fori_loop(0, NX * BLK, middle, 0)
    red_a2 = start([remote(mid_a.at[(x + d) % NX], last_a.at[x], along_x(d)) for d in (2, 1, 3)])
    red_b2 = start([remote(mid_b.at[(z + d) % NZ], last_b.at[z], along_z(d)) for d in (2, 1, 3)])
    sent += red_a2 + red_b2
    last_a[x] = mid_a[x]
    last_b[z] = mid_b[z]

    for copy in ret_hops[1] + ret_hops[3]:
        copy.wait_send()

    @pl.when(clip < 3)
    def _():
        move_tiles.wait_recv()

    get_hops = first_hop(tiles, SERVED, get_a, get_b)

    arrive(pool_a3)
    arrive(pool_b3)
    pool_4 = start([remote(every.at[c], every.at[c], along_x(0, 1))])
    sent += pool_4

    def total(buffer, at):
        value = buffer[(0, *at)].astype(F32)
        for n in range(1, 4):
            value = value + buffer[(n, *at)].astype(F32)
        return value

    arrive(red_a2)
    arrive(red_b2)
    for b in range(BLK):
        coarse[b, top] = total(last_a, (b,)).astype(BF16)
        coarse[b, bottom] = total(last_b, (b,)).astype(BF16)
    flip = (((0,), (0,)), ((), ()))
    for b in range(BLK):
        raw[b] = lax.dot_general(perm_ref[...], coarse[b], flip, preferred_element_type=F32).astype(BF16)

    for copy in share + red_1 + red_2:
        copy.wait_send()
    arrive(pool_4)
    load_every = start([here(every, partial)])
    load_every[0].wait()

    def query(n, carry):
        for t in range(4):
            m = 4 * n + t
            at = table[CTILE, m]
            tile = partial[at // (NX * NZ * BLK), (at // (NZ * BLK)) % NX, (at // BLK) % NZ, at % BLK]
            other[m] = (dot(other[m], tile) * scale).astype(BF16)
        return carry

    lax.fori_loop(0, TILES // 4, query, 0)

    get_far, near = second_hop(get_hops, get_a, get_b, got)
    sent += get_far

    arrive(ret_far)
    for copy in get_hops[1] + get_hops[3]:
        copy.wait_send()
    for copy in stay:
        copy.wait()
    load_back = start([here(back, slots)])
    load_back[0].wait()
    for part in range(4):
        rows = pl.ds(part * 64, 64)
        running[0] = jnp.zeros((64, PIX), F32)

        def add(n, value):
            for m in (4 * n, 4 * n + 1, 4 * n + 2, 4 * n + 3):
                value = value + slots[table[ORDER, m], rows].astype(F32)
                running[m + 1] = value
            return value

        lax.fori_loop(0, SLOTS // 4, add, jnp.zeros((64, PIX), F32))

        def gradient(n, carry):
            for t in range(8):
                m = 8 * n + t
                at = pl.ds(pl.multiple_of((m % 16) * SIDE, SIDE), SIDE)
                value = dot(widen_ref[rows], raw[m // 16, at]) * scale
                value = value + (running[table[FIRST, m + 1]] - running[table[FIRST, m]])
                terms[m, rows] = value.astype(BF16)
            return carry

        lax.fori_loop(0, TILES // 8, gradient, 0)

    arrive(get_far)
    for copy in near:
        copy.wait()

    def last(n, carry):
        for t in range(4):
            m = 4 * n + t
            value = dot(fine[m], got[table[GOT, m]]) * scale
            fine[m] = (value + other[m].astype(F32)).astype(BF16)
        return carry

    lax.fori_loop(0, TILES // 4, last, 0)

    for copy in sent:
        copy.wait_send()

    @pl.when(clip > 0)
    def _():
        move_pool.wait_send()
        move_tiles.wait_send()


def exchange(table, frames, tail, cot, base, frac):
    smem = pl.BlockSpec(memory_space=pltpu.SMEM)
    vmem = pl.BlockSpec(memory_space=pltpu.VMEM)
    hbm = pl.BlockSpec(memory_space=pl.ANY)
    tile = (PIX, PIX)
    shape = lambda *s: jax.ShapeDtypeStruct(s + tile, BF16)
    half = lambda *s: pltpu.VMEM(s + (HALF, PIX), BF16)
    full = lambda *s: pltpu.VMEM(s + tile, BF16)
    outs = pl.pallas_call(
        exchange_kernel,
        in_specs=[smem] + [vmem] * 6 + [hbm] * 3,
        out_specs=[vmem] * 2 + [hbm] * 6,
        out_shape=[
            full(TILES), full(TILES), shape(SLOTS), shape(NC, NX, NZ, BLK),
            shape(8, NX), shape(8, NZ), shape(8, NX), shape(8, NZ),
        ],
        scratch_shapes=[
            full(TILES + 1), pltpu.VMEM((TILES, 2, WIN * WIN, PIX), BF16),
            full(TILES), full(TILES), full(SLOTS), full(SLOTS),
            full(2, NX, NZ, BLK), full(NX, NZ, BLK), full(BLK), full(BLK), full(BLK),
            half(2, BLK), half(2, BLK), half(2, BLK), half(2, BLK),
            half(2, NX, BLK), half(2, NZ, BLK), half(NX, BLK), half(NZ, BLK),
            half(NX, BLK), half(NZ, BLK), full(BLK), pltpu.VMEM((SLOTS + 1, 64, PIX), F32),
            pltpu.SemaphoreType.DMA((80,)), pltpu.SemaphoreType.DMA((80,)),
            pltpu.SemaphoreType.DMA((24,)),
        ],
        compiler_params=pltpu.CompilerParams(
            collective_id=0, has_side_effects=True, vmem_limit_bytes=55 * 2**20),
        name="exchange",
    )(table, jnp.asarray(placement(), BF16), jnp.asarray(pool_rows(), BF16),
      jnp.asarray(block_rows(), BF16), jnp.asarray(pool_rows().T, BF16), base, frac, frames, tail, cot)
    return outs[:2]


def body(frames, tail, cotangent, window_base, window_frac, fine_owner, fine_local, coarse_owner, coarse_block):
    table = plan(*(v.reshape(8, 128) for v in (fine_owner, fine_local, coarse_owner, coarse_block)))
    grad_a, grad_b = exchange(table, frames[0], tail, cotangent[0], window_base[0], window_frac[0])
    return grad_a[None], grad_b[None]


def solution(mesh):
    in_specs = (
        P("clip", "space", None, None),
        P("space", None, None),
        P("clip", "space", None, None, None),
        P("clip", "space", None, None, None),
        P("clip", "space", None, None, None),
        P("clip", None, None),
        P("clip", None),
        P("clip", None, None),
        P("clip", None),
    )
    out_specs = (P("clip", "space", None, None), P("clip", "space", None, None))
    return jax.shard_map(body, mesh=mesh, in_specs=in_specs, out_specs=out_specs, check_vma=False)
```

```python
import functools

import jax
import jax.numpy as jnp
import numpy as np
from jax import lax
from jax.experimental import pallas as pl
from jax.experimental.pallas import tpu as pltpu
from jax.sharding import PartitionSpec as P

MESH = pl.DeviceIdType.MESH
POOL = 4
SIDE = 16
WIN = 9
PIX = 256
HALF = PIX // 2
NX, NZ, NC = 4, 4, 2
BLK = 2
TILES = 32
SLOTS = 2 * TILES
F32 = jnp.float32
BF16 = jnp.bfloat16


def placement():
    spread = np.zeros((2 * WIN * SIDE, WIN * WIN), np.float32)
    for a in range(WIN):
        for k in range(WIN):
            spread[a * SIDE + k, a * WIN + k] = 1
            spread[WIN * SIDE + a * SIDE + k + 1, a * WIN + k] = 1
    return spread


def pool_rows():
    rows = np.zeros((SIDE, PIX), np.float32)
    for y in range(SIDE):
        for x in range(SIDE):
            rows[(y // POOL) * POOL + x // POOL, y * SIDE + x] = 1
    return rows


def block_rows():
    rows = np.zeros((PIX, PIX), np.float32)
    for ty in range(4):
        for tx in range(4):
            for a in range(4):
                for b in range(4):
                    rows[(ty * 4 + a) * 16 + tx * 4 + b, (ty * 4 + tx) * 16 + a * 4 + b] = 1
    return rows


def dot(a, b):
    return jnp.dot(a, b, preferred_element_type=F32)


def window_map(spread, cot, base, frac):
    placed = dot(spread, cot)
    rows = WIN * SIDE
    fx = frac[0:1].astype(F32)
    fy = frac[1:2].astype(F32)
    shape = (SIDE, PIX)
    ox = jnp.broadcast_to(base[0:1] - WIN // 2, shape)
    oy = jnp.broadcast_to(base[1:2] - WIN // 2, shape)
    across = (1.0 - fx) * placed[:rows] + fx * placed[rows:]
    groups = []
    for y in range(WIN + 1):
        value = None
        if y < WIN:
            value = (1.0 - fy) * across[y * SIDE : (y + 1) * SIDE]
        if y > 0:
            below = fy * across[(y - 1) * SIDE : y * SIDE]
            value = below if value is None else value + below
        groups.append(value)
    for step in (1, 2, 4):
        chosen = (ox & step) != 0
        groups = [jnp.where(chosen, pltpu.roll(g, step, 0), g) for g in groups]
    zero = jnp.zeros(shape, F32)
    for step in (1, 2, 4):
        chosen = (oy & step) != 0
        count = min(SIDE, len(groups) + step)
        groups = [
            jnp.where(
                chosen,
                groups[y - step] if y >= step else zero,
                groups[y] if y < len(groups) else zero,
            )
            for y in range(count)
        ]
    return jnp.concatenate(groups, axis=0).astype(BF16)


def plan_kernel(owner_ref, local_ref, c_owner_ref, c_block_ref, out_ref):
    me = lax.axis_index("space")
    total = functools.partial(jnp.sum, keepdims=True)
    sub, lane = (lax.broadcasted_iota(jnp.int32, (TILES, TILES), n) for n in range(2))
    wide_sub, wide_lane = (lax.broadcasted_iota(jnp.int32, (TILES, SLOTS), n) for n in range(2))
    tall_sub, tall_lane = (lax.broadcasted_iota(jnp.int32, (SLOTS, TILES), n) for n in range(2))
    slot_sub, slot_lane = (lax.broadcasted_iota(jnp.int32, (SLOTS, SLOTS), n) for n in range(2))
    one = (sub == lane).astype(F32)
    row_of = lambda n: lax.broadcasted_iota(jnp.int32, (TILES, 128), n)
    per_row = 128 // TILES
    pick_row = (lax.broadcasted_iota(jnp.int32, (TILES, 8), 0) // per_row == lax.broadcasted_iota(jnp.int32, (TILES, 8), 1)).astype(F32)
    in_part = row_of(0) % per_row == row_of(1) // TILES
    fold = (lax.broadcasted_iota(jnp.int32, (128, TILES), 0) % TILES == lax.broadcasted_iota(jnp.int32, (128, TILES), 1)).astype(F32)

    def square(ref):
        rows = dot(pick_row, ref[...].astype(F32))
        return dot(jnp.where(in_part, rows, 0.0), fold).astype(jnp.int32)

    owner, local, c_owner, c_block = (square(r) for r in (owner_ref, local_ref, c_owner_ref, c_block_ref))
    flip = (((0,), (0,)), ((), ()))

    def turned(v):
        return lax.dot_general(v.astype(F32), one, flip, preferred_element_type=F32).astype(jnp.int32)

    def mine(v):
        row = total(jnp.where(sub == me, v, 0), axis=0)
        return row, total(jnp.where(lane == me, turned(v), 0), axis=1)

    def parts(v):
        return v // (NZ * NC), (v // NC) % NZ, v % NC

    own_row, own_col = mine(owner)
    same = own_row == own_col
    rank_row = total(jnp.where(same & (sub < lane), 1, 0), axis=0)
    rank_col = total(jnp.where(same & (lane < sub), 1, 0), axis=1)
    ox, oz, oc = parts(own_row)
    got_slot = jnp.where(rank_row == 0, (oz * NC + oc) * NX + ox, TILES + (ox * NC + oc) * NZ + oz)
    ox, oz, oc = parts(own_col)
    cross = (oc + me) % NC * 4
    ret_slot = jnp.where(rank_col == 0, ox * 8 + cross + oz, TILES + oz * 8 + cross + ox)
    filled = total(jnp.where(ret_slot == wide_lane, wide_sub, 0), axis=0)

    ctile_row, ctile_col = (
        ((o % NC) * (NX * NZ) + o // NC) * BLK + b for o, b in zip(mine(c_owner), mine(c_block)))
    named = ctile_col == wide_lane
    pick_a = jnp.min(jnp.where(named, wide_sub, TILES), axis=0, keepdims=True)
    pick_b = jnp.max(jnp.where(named, wide_sub, -1), axis=0, keepdims=True)
    pick_b = jnp.where((pick_b == pick_a) | (pick_b < 0), TILES, pick_b)

    def asked(hit, ids, earlier, axis):
        seen = hit.astype(F32)
        before = dot(earlier, seen) if axis == 0 else dot(seen, earlier)
        out = []
        for k in range(2):
            chosen = hit & (before.astype(jnp.int32) == k)
            value = total(jnp.where(chosen, ids, 0), axis=axis)
            count = total(jnp.where(chosen, 1, 0), axis=axis)
            out.append((value, jnp.where(count > 0, value, TILES)))
        return out

    (_, key0_row), (_, key1_row) = asked(turned(owner) == me, turned(local), (lane < sub).astype(F32), 0)
    (ask0, key0), (ask1, key1) = asked(owner == me, local, (sub < lane).astype(F32), 1)
    px, pz, pc = parts(wide_sub)
    cross = (pc + me) % NC * 4
    served = total(jnp.where(wide_lane == px * 8 + cross + pz, ask0, 0), axis=0)
    served += total(jnp.where(wide_lane == TILES + pz * 8 + cross + px, ask1, 0), axis=0)
    key_row = total(jnp.where(wide_lane == (pz * NC + pc) * NX + px, key0, 0), axis=0)
    key_row += total(jnp.where(wide_lane == TILES + (px * NC + pc) * NZ + pz, key1, 0), axis=0)
    px, pz, pc = parts(tall_lane)
    key_col = total(jnp.where(tall_sub == (pz * NC + pc) * NX + px, key0_row, 0), axis=1)
    key_col += total(jnp.where(tall_sub == TILES + (px * NC + pc) * NZ + pz, key1_row, 0), axis=1)
    ahead = (key_row < key_col) | ((key_row == key_col) & (slot_lane < slot_sub))
    place = total(jnp.where(ahead, 1, 0), axis=1)
    order = total(jnp.where(place == slot_lane, slot_sub, 0), axis=0)
    first = total(jnp.where(key_col < slot_lane, 1, 0), axis=0)
    out_ref[...] = jnp.zeros((8, SLOTS), jnp.int32)
    for row, value in enumerate((served, filled, pick_a, pick_b, ctile_row, got_slot, order, first)):
        out_ref[row : row + 1, : value.shape[1]] = value


SERVED, FILLED, PICK_A, PICK_B, CTILE, GOT, ORDER, FIRST = range(8)


def plan(*ids):
    vmem = pl.BlockSpec(memory_space=pltpu.VMEM)
    return pl.pallas_call(
        plan_kernel, in_specs=[vmem] * 4, out_specs=vmem,
        out_shape=jax.ShapeDtypeStruct((8, SLOTS), jnp.int32), name="plan",
    )(*ids)


def exchange_kernel(
    table, spread_ref, pool_ref, perm_ref, widen_ref, base, frac, frames, tail, cot_ref,
    fine, terms, other, got, back, every, ret_a, ret_b, get_a, get_b,
    first, cot, tiles, slots, partial, sibling, raw, pown, pbuf,
    up_a, down_a, up_b, down_b, red_a, red_b, mid_a, mid_b, last_a, last_b, coarse, running,
    send, recv, local
):
    scale = 1.0 / 16.0
    clip = lax.axis_index("clip")
    space = lax.axis_index("space")
    x = space // (NZ * NC)
    z = (space // NC) % NZ
    c = space % NC
    counts = {"remote": 0, "local": 0}

    def along_x(d, core=0):
        return (clip, (((x + d) % NX) * NZ + z) * NC + (c + core) % NC)

    def along_z(d, core=0):
        return (clip, (x * NZ + (z + d) % NZ) * NC + (c + core) % NC)

    def remote(src, dst, device):
        n = counts["remote"]
        counts["remote"] += 1
        return pltpu.make_async_remote_copy(
            src_ref=src, dst_ref=dst, send_sem=send.at[n], recv_sem=recv.at[n],
            device_id=device, device_id_type=MESH)

    def here(src, dst):
        n = counts["local"]
        counts["local"] += 1
        return pltpu.make_async_copy(src, dst, local.at[n])

    def start(copies):
        for copy in copies:
            copy.start()
        return copies

    def arrive(copies):
        for copy in copies:
            copy.wait_recv()

    load = start([here(frames, first.at[pl.ds(0, TILES)]), here(cot_ref, cot)])
    at_end = clip == 3
    below = ((clip + 3) % 4, space)
    move_tiles = remote(frames, tiles, below)
    end_tiles = here(tail, tiles)
    move_pool = remote(pown, pbuf, below)

    @pl.when(at_end)
    def _():
        end_tiles.start()

    barrier = pltpu.get_barrier_semaphore()
    greeted = [along_x(d, k) for d in range(1, NX) for k in range(NC)]
    greeted += [along_z(d, k) for d in range(1, NZ) for k in range(NC)]
    greeted += [along_x(0, 1), ((clip + 1) % 4, space)]
    for device in greeted:
        pl.semaphore_signal(barrier, inc=1, device_id=device, device_id_type=MESH)
    pl.semaphore_wait(barrier, len(greeted))

    sent = []

    def pool(source, target):
        def one(n, carry):
            for t in range(8):
                m = n * 8 + t
                rows = pl.ds(pl.multiple_of((m % 16) * SIDE, SIDE), SIDE)
                raw[m // 16, rows, :] = (dot(pool_ref[...], source[m]) * scale).astype(BF16)
            return carry
        lax.fori_loop(0, TILES // 8, one, 0)
        for b in range(BLK):
            target[b] = dot(perm_ref[...], raw[b]).astype(BF16)

    def products(begin, end, level, keep, put):
        def one(n, carry):
            for q in (2 * n, 2 * n + 1):
                weights = window_map(spread_ref[...], cot[q, :, level], base[q, level], frac[q, level])
                put[q] = (dot(weights, first[q]) * scale).astype(BF16)
                keep[q] = weights.T
            return carry
        lax.fori_loop(begin // 2, end // 2, one, 0)

    load[0].wait()
    pool(first, pown)

    @pl.when(clip > 0)
    def _():
        move_pool.start()

    @pl.when(at_end)
    def _():
        end_tiles.wait()
        pool(tiles, pbuf)

    load[1].wait()
    products(0, TILES // 4, 0, fine, terms)

    @pl.when(clip < 3)
    def _():
        move_pool.wait_recv()

    @pl.when(clip > 0)
    def _():
        move_tiles.start()

    top, bottom = pl.ds(0, HALF), pl.ds(HALF, HALF)
    keep_pool = start([here(pbuf, every.at[c, x, z])])
    pool_a1 = start([remote(pbuf.at[:, top], every.at[c, x, z, :, top], along_x(d)) for d in (2, 1, 3)])
    pool_b1 = start([remote(pbuf.at[:, bottom], every.at[c, x, z, :, bottom], along_z(d)) for d in (2, 1, 3)])
    sent += pool_a1 + pool_b1

    products(TILES // 4, TILES // 2, 0, fine, terms)

    keep_pool[0].wait()
    arrive(pool_a1)
    line = every.at[c, :, z, :, top]
    pool_a2 = start([remote(line, line, along_z(d)) for d in (1, NZ - 1)])
    arrive(pool_b1)
    line = every.at[c, x, :, :, bottom]
    pool_b2 = start([remote(line, line, along_x(d)) for d in (1, NX - 1)])
    sent += pool_a2 + pool_b2

    products(TILES // 2, TILES, 0, fine, terms)

    def fill_slots(half, source, row):
        def one(n, carry):
            for t in range(4):
                m = half * TILES + n * 4 + t
                slots[m] = source[table[row, m]]
            return carry
        lax.fori_loop(0, TILES // 4, one, 0)

    def group(half, n, k):
        return slots.at[pl.ds(half * TILES + n * 8 + k * 4, 4)]

    def first_hop(source, row, into_a, into_b):
        a, b = [], []
        for half, into, at, along, hops in ((0, into_a, x, along_x, a), (1, into_b, z, along_z, b)):
            fill_slots(half, source, row)
            for k in range(NC):
                part = into.at[pl.ds(k * 4, 4), at]
                far = start([remote(group(half, (at + d) % 4, k), part, along(d)) for d in (2, 1, 3)])
                hops.append((far, start([here(group(half, at, k), part)])))
        return a, b

    def first_sent(hops):
        for far, _ in hops[0] + hops[1]:
            for copy in far:
                copy.wait_send()

    def second_hop(hops, from_a, from_b, into):
        into_a = into.at[pl.ds((z * NC + c) * 4, 4)]
        into_b = into.at[pl.ds(TILES + (x * NC + c) * 4, 4)]
        far, near = [], []
        for k in range(NC):
            for hop, source, target, at, along in (
                (hops[0][k], from_a, into_a, z, along_z), (hops[1][k], from_b, into_b, x, along_x)):
                hop[1][0].wait()
                arrive(hop[0])
                far += start([remote(source.at[k * 4 + (at + d) % 4], target, along(d, k)) for d in (2, 1, 3)])
                if k == 0:
                    near += start([here(source.at[at], target)])
                else:
                    far += start([remote(source.at[4 + at], target, along(0, 1))])
        return far, near

    ret_hops = first_hop(terms, FILLED, ret_a, ret_b)

    products(0, TILES // 2, 1, other, first)

    x_up, x_down, z_up, z_down = (x + 1) % NX, (x + NX - 1) % NX, (z + 1) % NZ, (z + NZ - 1) % NZ
    low, high = pl.ds(0, 2), pl.ds(2, 2)
    arrive(pool_a2)
    line_up, line_down = every.at[c, low, z_down, :, top], every.at[c, high, z_up, :, top]
    pool_a3 = start([remote(line_up, line_up, along_z(1)), remote(line_down, line_down, along_z(NZ - 1))])
    arrive(pool_b2)
    line_up, line_down = every.at[c, x_down, low, :, bottom], every.at[c, x_up, high, :, bottom]
    pool_b3 = start([remote(line_up, line_up, along_x(1)), remote(line_down, line_down, along_x(NX - 1))])
    sent += pool_a3 + pool_b3

    products(TILES // 2, TILES, 1, other, first)
    first[TILES] = jnp.zeros((PIX, PIX), BF16)

    def fill(which, core):
        def one(n, carry):
            for t in range(4):
                m = 4 * n + t
                value = first[table[PICK_A, core * TILES + m]].astype(F32)
                value = value + first[table[PICK_B, core * TILES + m]].astype(F32)
                partial[which, m // (NZ * BLK), (m // BLK) % NZ, m % BLK] = value.astype(BF16)
            return carry
        lax.fori_loop(0, TILES // 4, one, 0)

    fill(1, 1 - c)
    share = start([remote(partial.at[1], sibling, along_x(0, 1))])
    fill(0, c)
    arrive(share)

    def join(n, carry):
        for t in range(4):
            m = 4 * n + t
            at = (m // (NZ * BLK), (m // BLK) % NZ, m % BLK)
            mine = partial[(0, *at)].astype(F32)
            partial[(0, *at)] = (mine + sibling[at].astype(F32)).astype(BF16)
        return carry

    lax.fori_loop(0, TILES // 4, join, 0)

    mine = partial.at[0]
    z_far, x_far = (z + 2) % NZ, (x + 2) % NX
    red_1 = start([
        remote(mine.at[low, z_far, :, top], up_a, along_z(1)),
        remote(mine.at[high, z_far, :, top], down_a, along_z(NZ - 1)),
        remote(mine.at[x_far, low, :, bottom], up_b, along_x(1)),
        remote(mine.at[x_far, high, :, bottom], down_b, along_x(NX - 1)),
    ])
    arrive(red_1)

    def pass_on(n, carry):
        i, b = n // BLK, n % BLK
        for at, extra in (
            ((0, i, z_up, b, top), up_a), ((0, i + 2, z_down, b, top), down_a),
            ((0, x_up, i, b, bottom), up_b), ((0, x_down, i + 2, b, bottom), down_b),
        ):
            partial[at] = (partial[at].astype(F32) + extra[i, b].astype(F32)).astype(BF16)
        return carry

    lax.fori_loop(0, 2 * BLK, pass_on, 0)
    red_2 = start([
        remote(mine.at[:, z_up, :, top], red_a.at[0], along_z(1)),
        remote(mine.at[:, z_down, :, top], red_a.at[1], along_z(NZ - 1)),
        remote(mine.at[x_up, :, :, bottom], red_b.at[0], along_x(1)),
        remote(mine.at[x_down, :, :, bottom], red_b.at[1], along_x(NX - 1)),
    ])

    ret_far, stay = second_hop(ret_hops, ret_a, ret_b, back)
    sent += ret_far

    arrive(red_2)

    def middle(n, carry):
        i, b = n // BLK, n % BLK
        for at, extra, into in (((0, i, z, b, top), red_a, mid_a), ((0, x, i, b, bottom), red_b, mid_b)):
            value = partial[at].astype(F32) + extra[0, i, b].astype(F32) + extra[1, i, b].astype(F32)
            into[i, b] = value.astype(BF16)
        return carry

    lax.fori_loop(0, NX * BLK, middle, 0)
    red_a2 = start([remote(mid_a.at[(x + d) % NX], last_a.at[x], along_x(d)) for d in (2, 1, 3)])
    red_b2 = start([remote(mid_b.at[(z + d) % NZ], last_b.at[z], along_z(d)) for d in (2, 1, 3)])
    sent += red_a2 + red_b2
    last_a[x] = mid_a[x]
    last_b[z] = mid_b[z]

    first_sent(ret_hops)

    @pl.when(clip < 3)
    def _():
        move_tiles.wait_recv()

    get_hops = first_hop(tiles, SERVED, get_a, get_b)

    arrive(pool_a3)
    arrive(pool_b3)
    pool_4 = start([remote(every.at[c], every.at[c], along_x(0, 1))])
    sent += pool_4

    def total(buffer, at):
        value = buffer[(0, *at)].astype(F32)
        for n in range(1, 4):
            value = value + buffer[(n, *at)].astype(F32)
        return value

    arrive(red_a2)
    arrive(red_b2)
    for b in range(BLK):
        coarse[b, top] = total(last_a, (b,)).astype(BF16)
        coarse[b, bottom] = total(last_b, (b,)).astype(BF16)
    flip = (((0,), (0,)), ((), ()))
    for b in range(BLK):
        raw[b] = lax.dot_general(perm_ref[...], coarse[b], flip, preferred_element_type=F32).astype(BF16)

    for copy in share + red_1 + red_2:
        copy.wait_send()
    arrive(pool_4)
    load_every = start([here(every, partial)])
    load_every[0].wait()

    def query(n, carry):
        for t in range(4):
            m = 4 * n + t
            at = table[CTILE, m]
            tile = partial[at // (NX * NZ * BLK), (at // (NZ * BLK)) % NX, (at // BLK) % NZ, at % BLK]
            other[m] = (dot(other[m], tile) * scale).astype(BF16)
        return carry

    lax.fori_loop(0, TILES // 4, query, 0)

    get_far, near = second_hop(get_hops, get_a, get_b, got)
    sent += get_far

    arrive(ret_far)
    first_sent(get_hops)
    for copy in stay:
        copy.wait()
    load_back = start([here(back, slots)])
    load_back[0].wait()
    for part in range(4):
        rows = pl.ds(part * 64, 64)
        running[0] = jnp.zeros((64, PIX), F32)

        def add(n, value):
            for m in (4 * n, 4 * n + 1, 4 * n + 2, 4 * n + 3):
                value = value + slots[table[ORDER, m], rows].astype(F32)
                running[m + 1] = value
            return value

        lax.fori_loop(0, SLOTS // 4, add, jnp.zeros((64, PIX), F32))

        def gradient(n, carry):
            for t in range(8):
                m = 8 * n + t
                at = pl.ds(pl.multiple_of((m % 16) * SIDE, SIDE), SIDE)
                value = dot(widen_ref[rows], raw[m // 16, at]) * scale
                value = value + (running[table[FIRST, m + 1]] - running[table[FIRST, m]])
                terms[m, rows] = value.astype(BF16)
            return carry

        lax.fori_loop(0, TILES // 8, gradient, 0)

    arrive(get_far)
    for copy in near:
        copy.wait()
    for copy in sent:
        copy.wait_send()

    @pl.when(clip > 0)
    def _():
        move_pool.wait_send()
        move_tiles.wait_send()


def exchange(table, frames, tail, cot, base, frac):
    smem = pl.BlockSpec(memory_space=pltpu.SMEM)
    vmem = pl.BlockSpec(memory_space=pltpu.VMEM)
    hbm = pl.BlockSpec(memory_space=pl.ANY)
    tile = (PIX, PIX)
    shape = lambda *s: jax.ShapeDtypeStruct(s + tile, BF16)
    half = lambda *s: pltpu.VMEM(s + (HALF, PIX), BF16)
    full = lambda *s: pltpu.VMEM(s + tile, BF16)
    outs = pl.pallas_call(
        exchange_kernel,
        in_specs=[smem] + [vmem] * 6 + [hbm] * 3,
        out_specs=[vmem] * 4 + [hbm] * 6,
        out_shape=[
            full(TILES), full(TILES), full(TILES), full(SLOTS), shape(SLOTS), shape(NC, NX, NZ, BLK),
            shape(8, NX), shape(8, NZ), shape(8, NX), shape(8, NZ),
        ],
        scratch_shapes=[
            full(TILES + 1), pltpu.VMEM((TILES, WIN * WIN, 2, PIX), BF16),
            full(TILES), full(SLOTS),
            full(2, NX, NZ, BLK), full(NX, NZ, BLK), full(BLK), full(BLK), full(BLK),
            half(2, BLK), half(2, BLK), half(2, BLK), half(2, BLK),
            half(2, NX, BLK), half(2, NZ, BLK), half(NX, BLK), half(NZ, BLK),
            half(NX, BLK), half(NZ, BLK), full(BLK), pltpu.VMEM((SLOTS + 1, 64, PIX), F32),
            pltpu.SemaphoreType.DMA((100,)), pltpu.SemaphoreType.DMA((100,)),
            pltpu.SemaphoreType.DMA((32,)),
        ],
        compiler_params=pltpu.CompilerParams(
            collective_id=0, has_side_effects=True, vmem_limit_bytes=43 * 2**20),
        name="exchange",
    )(table, jnp.asarray(placement(), BF16), jnp.asarray(pool_rows(), BF16),
      jnp.asarray(block_rows(), BF16), jnp.asarray(pool_rows().T, BF16), base, frac, frames, tail, cot)
    return outs[:4]


def finish_kernel(table, fine, terms, other, got, grad_a, grad_b, ready, done):
    second = pltpu.make_async_copy(terms, grad_b, done.at[TILES // GROUP])
    second.start()
    copies = []
    for g in range(TILES // GROUP):
        for n in range(g * GROUP, (g + 1) * GROUP):
            value = dot(fine[n], got[table[GOT, n]]) * (1.0 / 16.0)
            ready[n] = (value + other[n].astype(F32)).astype(BF16)
        rows = pl.ds(g * GROUP, GROUP)
        copies.append(pltpu.make_async_copy(ready.at[rows], grad_a.at[rows], done.at[g]))
        copies[-1].start()
    for copy in copies:
        copy.wait()
    second.wait()


GROUP = 4


def finish(table, *parts):
    vmem = pl.BlockSpec(memory_space=pltpu.VMEM)
    out = jax.ShapeDtypeStruct((TILES, PIX, PIX), BF16)
    return pl.pallas_call(
        finish_kernel,
        in_specs=[pl.BlockSpec(memory_space=pltpu.SMEM)] + [vmem] * 4,
        out_specs=[pl.BlockSpec(memory_space=pl.ANY)] * 2,
        out_shape=[out, out],
        scratch_shapes=[pltpu.VMEM((TILES, PIX, PIX), BF16), pltpu.SemaphoreType.DMA((TILES // GROUP + 1,))],
        compiler_params=pltpu.CompilerParams(vmem_limit_bytes=30 * 2**20),
        name="finish",
    )(table, *parts)


def body(frames, tail, cotangent, window_base, window_frac, fine_owner, fine_local, coarse_owner, coarse_block):
    table = plan(*(v.reshape(8, 128) for v in (fine_owner, fine_local, coarse_owner, coarse_block)))
    parts = exchange(table, frames[0], tail, cotangent[0].transpose(0, 2, 1, 3), window_base[0], window_frac[0])
    grad_a, grad_b = finish(table, *parts)
    return grad_a[None], grad_b[None]


def solution(mesh):
    in_specs = (
        P("clip", "space", None, None),
        P("space", None, None),
        P("clip", "space", None, None, None),
        P("clip", "space", None, None, None),
        P("clip", "space", None, None, None),
        P("clip", None, None),
        P("clip", None),
        P("clip", None, None),
        P("clip", None),
    )
    out_specs = (P("clip", "space", None, None), P("clip", "space", None, None))
    return jax.shard_map(body, mesh=mesh, in_specs=in_specs, out_specs=out_specs, check_vma=False)
```

```python
import functools

import jax
import jax.numpy as jnp
import numpy as np
from jax import lax
from jax.experimental import pallas as pl
from jax.experimental.pallas import tpu as pltpu
from jax.sharding import PartitionSpec as P

MESH = pl.DeviceIdType.MESH
POOL = 4
SIDE = 16
WIN = 9
PIX = 256
HALF = PIX // 2
NX, NZ, NC = 4, 4, 2
BLK = 2
TILES = 32
SLOTS = 2 * TILES
F32 = jnp.float32
BF16 = jnp.bfloat16


def placement():
    spread = np.zeros((2 * WIN * SIDE, WIN * WIN), np.float32)
    for a in range(WIN):
        for k in range(WIN):
            spread[a * SIDE + k, a * WIN + k] = 1
            spread[WIN * SIDE + a * SIDE + k + 1, a * WIN + k] = 1
    return spread


def pool_rows():
    rows = np.zeros((SIDE, PIX), np.float32)
    for y in range(SIDE):
        for x in range(SIDE):
            rows[(y // POOL) * POOL + x // POOL, y * SIDE + x] = 1
    return rows


def block_rows():
    rows = np.zeros((PIX, PIX), np.float32)
    for ty in range(4):
        for tx in range(4):
            for a in range(4):
                for b in range(4):
                    rows[(ty * 4 + a) * 16 + tx * 4 + b, (ty * 4 + tx) * 16 + a * 4 + b] = 1
    return rows


def dot(a, b):
    return jnp.dot(a, b, preferred_element_type=F32)


def window_map(spread, cot, base, frac):
    placed = dot(spread, cot)
    rows = WIN * SIDE
    fx = frac[0:1].astype(F32)
    fy = frac[1:2].astype(F32)
    shape = (SIDE, PIX)
    ox = jnp.broadcast_to(base[0:1] - WIN // 2, shape)
    oy = jnp.broadcast_to(base[1:2] - WIN // 2, shape)
    across = (1.0 - fx) * placed[:rows] + fx * placed[rows:]
    groups = []
    for y in range(WIN + 1):
        value = None
        if y < WIN:
            value = (1.0 - fy) * across[y * SIDE : (y + 1) * SIDE]
        if y > 0:
            below = fy * across[(y - 1) * SIDE : y * SIDE]
            value = below if value is None else value + below
        groups.append(value)
    for step in (1, 2, 4):
        chosen = (ox & step) != 0
        groups = [jnp.where(chosen, pltpu.roll(g, step, 0), g) for g in groups]
    zero = jnp.zeros(shape, F32)
    for step in (1, 2, 4):
        chosen = (oy & step) != 0
        count = min(SIDE, len(groups) + step)
        groups = [
            jnp.where(
                chosen,
                groups[y - step] if y >= step else zero,
                groups[y] if y < len(groups) else zero,
            )
            for y in range(count)
        ]
    return jnp.concatenate(groups, axis=0).astype(BF16)


def make_table(owner_ref, local_ref, c_owner_ref, c_block_ref, out_ref):
    me = lax.axis_index("space")
    total = functools.partial(jnp.sum, keepdims=True)
    sub, lane = (lax.broadcasted_iota(jnp.int32, (TILES, TILES), n) for n in range(2))
    wide_sub, wide_lane = (lax.broadcasted_iota(jnp.int32, (TILES, SLOTS), n) for n in range(2))
    tall_sub, tall_lane = (lax.broadcasted_iota(jnp.int32, (SLOTS, TILES), n) for n in range(2))
    slot_sub, slot_lane = (lax.broadcasted_iota(jnp.int32, (SLOTS, SLOTS), n) for n in range(2))
    one = (sub == lane).astype(F32)
    row_of = lambda n: lax.broadcasted_iota(jnp.int32, (TILES, 128), n)
    per_row = 128 // TILES
    pick_row = (lax.broadcasted_iota(jnp.int32, (TILES, 8), 0) // per_row == lax.broadcasted_iota(jnp.int32, (TILES, 8), 1)).astype(F32)
    in_part = row_of(0) % per_row == row_of(1) // TILES
    fold = (lax.broadcasted_iota(jnp.int32, (128, TILES), 0) % TILES == lax.broadcasted_iota(jnp.int32, (128, TILES), 1)).astype(F32)

    def square(ref):
        rows = dot(pick_row, ref[...].astype(F32))
        return dot(jnp.where(in_part, rows, 0.0), fold).astype(jnp.int32)

    owner, local, c_owner, c_block = (square(r) for r in (owner_ref, local_ref, c_owner_ref, c_block_ref))
    flip = (((0,), (0,)), ((), ()))

    def turned(v):
        return lax.dot_general(v.astype(F32), one, flip, preferred_element_type=F32).astype(jnp.int32)

    def mine(v):
        row = total(jnp.where(sub == me, v, 0), axis=0)
        return row, total(jnp.where(lane == me, turned(v), 0), axis=1)

    def parts(v):
        return v // (NZ * NC), (v // NC) % NZ, v % NC

    own_row, own_col = mine(owner)
    same = own_row == own_col
    rank_row = total(jnp.where(same & (sub < lane), 1, 0), axis=0)
    rank_col = total(jnp.where(same & (lane < sub), 1, 0), axis=1)
    ox, oz, oc = parts(own_row)
    got_slot = jnp.where(rank_row == 0, (oz * NC + oc) * NX + ox, TILES + (ox * NC + oc) * NZ + oz)
    ox, oz, oc = parts(own_col)
    cross = (oc + me) % NC * 4
    ret_slot = jnp.where(rank_col == 0, ox * 8 + cross + oz, TILES + oz * 8 + cross + ox)
    filled = jnp.max(jnp.where(ret_slot == wide_lane, wide_sub, 0), axis=0, keepdims=True)

    ctile_row, ctile_col = (
        ((o % NC) * (NX * NZ) + o // NC) * BLK + b for o, b in zip(mine(c_owner), mine(c_block)))
    named = ctile_col == wide_lane
    pick_a = jnp.min(jnp.where(named, wide_sub, TILES), axis=0, keepdims=True)
    pick_b = jnp.max(jnp.where(named, wide_sub, -1), axis=0, keepdims=True)
    pick_b = jnp.where((pick_b == pick_a) | (pick_b < 0), TILES, pick_b)

    def asked(hit, ids, earlier, axis):
        seen = hit.astype(F32)
        before = dot(earlier, seen) if axis == 0 else dot(seen, earlier)
        out = []
        for k in range(2):
            chosen = hit & (before.astype(jnp.int32) == k)
            value = total(jnp.where(chosen, ids, 0), axis=axis)
            count = total(jnp.where(chosen, 1, 0), axis=axis)
            out.append((value, jnp.where(count > 0, value, TILES)))
        return out

    (_, key0_row), (_, key1_row) = asked(turned(owner) == me, turned(local), (lane < sub).astype(F32), 0)
    (ask0, key0), (ask1, key1) = asked(owner == me, local, (sub < lane).astype(F32), 1)
    px, pz, pc = parts(wide_sub)
    cross = (pc + me) % NC * 4
    served = total(jnp.where(wide_lane == px * 8 + cross + pz, ask0, 0), axis=0)
    served += total(jnp.where(wide_lane == TILES + pz * 8 + cross + px, ask1, 0), axis=0)
    key_row = total(jnp.where(wide_lane == (pz * NC + pc) * NX + px, key0, 0), axis=0)
    key_row += total(jnp.where(wide_lane == TILES + (px * NC + pc) * NZ + pz, key1, 0), axis=0)
    px, pz, pc = parts(tall_lane)
    key_col = total(jnp.where(tall_sub == (pz * NC + pc) * NX + px, key0_row, 0), axis=1)
    key_col += total(jnp.where(tall_sub == TILES + (px * NC + pc) * NZ + pz, key1_row, 0), axis=1)
    ahead = (key_row < key_col) | ((key_row == key_col) & (slot_lane < slot_sub))
    place = total(jnp.where(ahead, 1, 0), axis=1)
    order = total(jnp.where(place == slot_lane, slot_sub, 0), axis=0)
    first = total(jnp.where(key_col < slot_lane, 1, 0), axis=0)
    out_ref[...] = jnp.zeros((8, SLOTS), jnp.int32)
    rows = (served, filled, pick_a, pick_b, ctile_row, got_slot, order, first)
    tops = (TILES - 1, TILES - 1, TILES, TILES, SLOTS - 1, SLOTS - 1, SLOTS - 1, SLOTS)
    for row, (value, top) in enumerate(zip(rows, tops)):
        out_ref[row : row + 1, : value.shape[1]] = jnp.clip(value, 0, top)


SERVED, FILLED, PICK_A, PICK_B, CTILE, GOT, ORDER, FIRST = range(8)


def exchange_kernel(
    owner, local_id, c_owner, c_block, spread_ref, pool_ref, perm_ref, widen_ref, base, frac, frames, tail, cot_ref,
    fine, terms, other, got, rows_of, back, every, below_every, ret_a, ret_b, get_a, get_b,
    first, cot, tiles, slots, partial, sibling, raw, pbuf,
    up_a, down_a, up_b, down_b, red_a, red_b, mid_a, mid_b, last_a, last_b, coarse, running, table,
    send, recv, local
):
    scale = 1.0 / 16.0
    clip = lax.axis_index("clip")
    space = lax.axis_index("space")
    x = space // (NZ * NC)
    z = (space // NC) % NZ
    c = space % NC
    counts = {"remote": 0, "local": 0}

    def along_x(d, core=0):
        return (clip, (((x + d) % NX) * NZ + z) * NC + (c + core) % NC)

    def along_z(d, core=0):
        return (clip, (x * NZ + (z + d) % NZ) * NC + (c + core) % NC)

    def remote(src, dst, device):
        n = counts["remote"]
        counts["remote"] += 1
        return pltpu.make_async_remote_copy(
            src_ref=src, dst_ref=dst, send_sem=send.at[n], recv_sem=recv.at[n],
            device_id=device, device_id_type=MESH)

    def here(src, dst):
        n = counts["local"]
        counts["local"] += 1
        return pltpu.make_async_copy(src, dst, local.at[n])

    def start(copies):
        for copy in copies:
            copy.start()
        return copies

    def arrive(copies):
        for copy in copies:
            copy.wait_recv()

    load = start([here(frames, first.at[pl.ds(0, TILES)]), here(cot_ref, cot)])
    at_end = clip == 3
    below = ((clip + 3) % 4, space)
    move_tiles = remote(frames, tiles, below)
    end_tiles = here(tail, tiles)
    pool_tail = here(tail, slots.at[pl.ds(0, TILES)])

    @pl.when(at_end)
    def _():
        end_tiles.start()

    @pl.when(clip == 0)
    def _():
        pool_tail.start()

    barrier = pltpu.get_barrier_semaphore()
    greeted = [along_x(d, k) for d in range(1, NX) for k in range(NC)]
    greeted += [along_z(d, k) for d in range(1, NZ) for k in range(NC)]
    greeted += [along_x(0, 1), ((clip + 1) % 4, space)]
    for device in greeted:
        pl.semaphore_signal(barrier, inc=1, device_id=device, device_id_type=MESH)
    pl.semaphore_wait(barrier, len(greeted))

    sent = []

    @pl.when(clip > 0)
    def _():
        move_tiles.start()

    def pool(source, target):
        def one(n, carry):
            for t in range(8):
                m = n * 8 + t
                rows = pl.ds(pl.multiple_of((m % 16) * SIDE, SIDE), SIDE)
                raw[m // 16, rows, :] = (dot(pool_ref[...], source[m]) * scale).astype(BF16)
            return carry
        lax.fori_loop(0, TILES // 8, one, 0)
        for b in range(BLK):
            target[b] = dot(perm_ref[...], raw[b]).astype(BF16)

    def products(begin, end, level, keep, put):
        def one(n, carry):
            for q in (2 * n, 2 * n + 1):
                weights = window_map(spread_ref[...], cot[q, :, level], base[q, level], frac[q, level])
                put[q] = (dot(weights, first[q]) * scale).astype(BF16)
                keep[q] = weights.T
            return carry
        lax.fori_loop(begin // 2, end // 2, one, 0)

    load[0].wait()

    @pl.when(clip > 0)
    def _():
        pool(first, pbuf)

    @pl.when(clip == 0)
    def _():
        pool_tail.wait()
        pool(slots, pbuf)

    top, bottom = pl.ds(0, HALF), pl.ds(HALF, HALF)
    keep_pool = start([here(pbuf, every.at[c, x, z])])
    pool_a1 = start([remote(pbuf.at[:, top], every.at[c, x, z, :, top], along_x(d)) for d in (2, 1, 3)])
    pool_b1 = start([remote(pbuf.at[:, bottom], every.at[c, x, z, :, bottom], along_z(d)) for d in (2, 1, 3)])
    sent += pool_a1 + pool_b1

    make_table(owner, local_id, c_owner, c_block, rows_of)
    load_table = start([here(rows_of, table)])
    load[1].wait()
    products(0, TILES // 2, 0, fine, terms)
    load_table[0].wait()

    keep_pool[0].wait()
    arrive(pool_a1)
    line = every.at[c, :, z, :, top]
    pool_a2 = start([remote(line, line, along_z(d)) for d in (1, NZ - 1)])
    arrive(pool_b1)
    line = every.at[c, x, :, :, bottom]
    pool_b2 = start([remote(line, line, along_x(d)) for d in (1, NX - 1)])
    sent += pool_a2 + pool_b2

    products(TILES // 2, TILES, 0, fine, terms)

    def fill_slots(half, source, row):
        def one(n, carry):
            for t in range(4):
                m = half * TILES + n * 4 + t
                slots[m] = source[table[row, m]]
            return carry
        lax.fori_loop(0, TILES // 4, one, 0)

    def group(half, n, k):
        return slots.at[pl.ds(half * TILES + n * 8 + k * 4, 4)]

    def first_hop(source, row, into_a, into_b):
        a, b = [], []
        for half, into, at, along, hops in ((0, into_a, x, along_x, a), (1, into_b, z, along_z, b)):
            fill_slots(half, source, row)
            for k in range(NC):
                part = into.at[pl.ds(k * 4, 4), at]
                far = start([remote(group(half, (at + d) % 4, k), part, along(d)) for d in (2, 1, 3)])
                hops.append((far, start([here(group(half, at, k), part)])))
        return a, b

    def first_sent(hops):
        for far, _ in hops[0] + hops[1]:
            for copy in far:
                copy.wait_send()

    def second_hop(hops, from_a, from_b, into):
        into_a = into.at[pl.ds((z * NC + c) * 4, 4)]
        into_b = into.at[pl.ds(TILES + (x * NC + c) * 4, 4)]
        far, near = [], []
        for k in range(NC):
            for hop, source, target, at, along in (
                (hops[0][k], from_a, into_a, z, along_z), (hops[1][k], from_b, into_b, x, along_x)):
                hop[1][0].wait()
                arrive(hop[0])
                far += start([remote(source.at[k * 4 + (at + d) % 4], target, along(d, k)) for d in (2, 1, 3)])
                if k == 0:
                    near += start([here(source.at[at], target)])
                else:
                    far += start([remote(source.at[4 + at], target, along(0, 1))])
        return far, near

    ret_hops = first_hop(terms, FILLED, ret_a, ret_b)

    products(0, TILES // 2, 1, other, first)

    x_up, x_down, z_up, z_down = (x + 1) % NX, (x + NX - 1) % NX, (z + 1) % NZ, (z + NZ - 1) % NZ
    low, high = pl.ds(0, 2), pl.ds(2, 2)
    arrive(pool_a2)
    line_up, line_down = every.at[c, low, z_down, :, top], every.at[c, high, z_up, :, top]
    pool_a3 = start([remote(line_up, line_up, along_z(1)), remote(line_down, line_down, along_z(NZ - 1))])
    arrive(pool_b2)
    line_up, line_down = every.at[c, x_down, low, :, bottom], every.at[c, x_up, high, :, bottom]
    pool_b3 = start([remote(line_up, line_up, along_x(1)), remote(line_down, line_down, along_x(NX - 1))])
    sent += pool_a3 + pool_b3

    products(TILES // 2, TILES, 1, other, first)
    first[TILES] = jnp.zeros((PIX, PIX), BF16)

    def fill(which, core):
        def one(n, carry):
            for t in range(4):
                m = 4 * n + t
                value = first[table[PICK_A, core * TILES + m]].astype(F32)
                value = value + first[table[PICK_B, core * TILES + m]].astype(F32)
                partial[which, m // (NZ * BLK), (m // BLK) % NZ, m % BLK] = value.astype(BF16)
            return carry
        lax.fori_loop(0, TILES // 4, one, 0)

    fill(1, 1 - c)
    share = start([remote(partial.at[1], sibling, along_x(0, 1))])
    fill(0, c)
    arrive(share)

    def join(n, carry):
        for t in range(4):
            m = 4 * n + t
            at = (m // (NZ * BLK), (m // BLK) % NZ, m % BLK)
            mine = partial[(0, *at)].astype(F32)
            partial[(0, *at)] = (mine + sibling[at].astype(F32)).astype(BF16)
        return carry

    lax.fori_loop(0, TILES // 4, join, 0)

    mine = partial.at[0]
    z_far, x_far = (z + 2) % NZ, (x + 2) % NX
    red_1 = start([
        remote(mine.at[low, z_far, :, top], up_a, along_z(1)),
        remote(mine.at[high, z_far, :, top], down_a, along_z(NZ - 1)),
        remote(mine.at[x_far, low, :, bottom], up_b, along_x(1)),
        remote(mine.at[x_far, high, :, bottom], down_b, along_x(NX - 1)),
    ])
    arrive(red_1)

    def pass_on(n, carry):
        i, b = n // BLK, n % BLK
        for at, extra in (
            ((0, i, z_up, b, top), up_a), ((0, i + 2, z_down, b, top), down_a),
            ((0, x_up, i, b, bottom), up_b), ((0, x_down, i + 2, b, bottom), down_b),
        ):
            partial[at] = (partial[at].astype(F32) + extra[i, b].astype(F32)).astype(BF16)
        return carry

    lax.fori_loop(0, 2 * BLK, pass_on, 0)
    red_2 = start([
        remote(mine.at[:, z_up, :, top], red_a.at[0], along_z(1)),
        remote(mine.at[:, z_down, :, top], red_a.at[1], along_z(NZ - 1)),
        remote(mine.at[x_up, :, :, bottom], red_b.at[0], along_x(1)),
        remote(mine.at[x_down, :, :, bottom], red_b.at[1], along_x(NX - 1)),
    ])

    arrive(pool_a3)
    arrive(pool_b3)
    pool_4 = start([remote(every.at[c], below_every.at[c], below)])

    ret_far, stay = second_hop(ret_hops, ret_a, ret_b, back)
    sent += ret_far

    arrive(red_2)

    def middle(n, carry):
        i, b = n // BLK, n % BLK
        for at, extra, into in (((0, i, z, b, top), red_a, mid_a), ((0, x, i, b, bottom), red_b, mid_b)):
            value = partial[at].astype(F32) + extra[0, i, b].astype(F32) + extra[1, i, b].astype(F32)
            into[i, b] = value.astype(BF16)
        return carry

    lax.fori_loop(0, NX * BLK, middle, 0)
    red_a2 = start([remote(mid_a.at[(x + d) % NX], last_a.at[x], along_x(d)) for d in (2, 1, 3)])
    red_b2 = start([remote(mid_b.at[(z + d) % NZ], last_b.at[z], along_z(d)) for d in (2, 1, 3)])
    sent += red_a2 + red_b2
    last_a[x] = mid_a[x]
    last_b[z] = mid_b[z]

    first_sent(ret_hops)

    @pl.when(at_end)
    def _():
        end_tiles.wait()

    @pl.when(clip < 3)
    def _():
        move_tiles.wait_recv()

    get_hops = first_hop(tiles, SERVED, get_a, get_b)

    def total(buffer, at):
        value = buffer[(0, *at)].astype(F32)
        for n in range(1, 4):
            value = value + buffer[(n, *at)].astype(F32)
        return value

    arrive(red_a2)
    arrive(red_b2)
    for b in range(BLK):
        coarse[b, top] = total(last_a, (b,)).astype(BF16)
        coarse[b, bottom] = total(last_b, (b,)).astype(BF16)
    flip = (((0,), (0,)), ((), ()))
    for b in range(BLK):
        raw[b] = lax.dot_general(perm_ref[...], coarse[b], flip, preferred_element_type=F32).astype(BF16)

    get_far, near = second_hop(get_hops, get_a, get_b, got)
    sent += get_far

    arrive(ret_far)
    first_sent(get_hops)
    for copy in stay:
        copy.wait()
    load_back = start([here(back, slots)])
    load_back[0].wait()
    for part in range(4):
        rows = pl.ds(part * 64, 64)
        running[0] = jnp.zeros((64, PIX), F32)

        def add(n, value):
            for m in (4 * n, 4 * n + 1, 4 * n + 2, 4 * n + 3):
                value = value + slots[table[ORDER, m], rows].astype(F32)
                running[m + 1] = value
            return value

        lax.fori_loop(0, SLOTS // 4, add, jnp.zeros((64, PIX), F32))

        def gradient(n, carry):
            for t in range(8):
                m = 8 * n + t
                at = pl.ds(pl.multiple_of((m % 16) * SIDE, SIDE), SIDE)
                value = dot(widen_ref[rows], raw[m // 16, at]) * scale
                value = value + (running[table[FIRST, m + 1]] - running[table[FIRST, m]])
                terms[m, rows] = value.astype(BF16)
            return carry

        lax.fori_loop(0, TILES // 8, gradient, 0)

    arrive(pool_4)
    pool_5 = start([remote(below_every.at[c], below_every.at[c], along_x(0, 1))])
    sent += pool_4 + pool_5
    for copy in share + red_1 + red_2:
        copy.wait_send()
    arrive(pool_5)
    load_every = start([here(below_every, partial)])
    load_every[0].wait()

    def query(n, carry):
        for t in range(4):
            m = 4 * n + t
            at = table[CTILE, m]
            tile = partial[at // (NX * NZ * BLK), (at // (NZ * BLK)) % NX, (at // BLK) % NZ, at % BLK]
            other[m] = (dot(other[m], tile) * scale).astype(BF16)
        return carry

    lax.fori_loop(0, TILES // 4, query, 0)

    arrive(get_far)
    for copy in near:
        copy.wait()
    for copy in sent:
        copy.wait_send()

    @pl.when(clip > 0)
    def _():
        move_tiles.wait_send()


def exchange(ids, frames, tail, cot, base, frac):
    vmem = pl.BlockSpec(memory_space=pltpu.VMEM)
    hbm = pl.BlockSpec(memory_space=pl.ANY)
    tile = (PIX, PIX)
    shape = lambda *s: jax.ShapeDtypeStruct(s + tile, BF16)
    half = lambda *s: pltpu.VMEM(s + (HALF, PIX), BF16)
    full = lambda *s: pltpu.VMEM(s + tile, BF16)
    outs = pl.pallas_call(
        exchange_kernel,
        in_specs=[vmem] * 10 + [hbm] * 3,
        out_specs=[vmem] * 5 + [hbm] * 7,
        out_shape=[
            full(TILES), full(TILES), full(TILES), full(SLOTS),
            pltpu.VMEM((8, SLOTS), jnp.int32), shape(SLOTS), shape(NC, NX, NZ, BLK), shape(NC, NX, NZ, BLK),
            shape(8, NX), shape(8, NZ), shape(8, NX), shape(8, NZ),
        ],
        scratch_shapes=[
            full(TILES + 1), pltpu.VMEM((TILES, WIN * WIN, 2, PIX), BF16),
            full(TILES), full(SLOTS),
            full(2, NX, NZ, BLK), full(NX, NZ, BLK), full(BLK), full(BLK),
            half(2, BLK), half(2, BLK), half(2, BLK), half(2, BLK),
            half(2, NX, BLK), half(2, NZ, BLK), half(NX, BLK), half(NZ, BLK),
            half(NX, BLK), half(NZ, BLK), full(BLK), pltpu.VMEM((SLOTS + 1, 64, PIX), F32),
            pltpu.SMEM((8, SLOTS), jnp.int32),
            pltpu.SemaphoreType.DMA((100,)), pltpu.SemaphoreType.DMA((100,)),
            pltpu.SemaphoreType.DMA((32,)),
        ],
        compiler_params=pltpu.CompilerParams(
            collective_id=0, has_side_effects=True, vmem_limit_bytes=43 * 2**20),
        name="exchange",
    )(*ids, jnp.asarray(placement(), BF16), jnp.asarray(pool_rows(), BF16),
      jnp.asarray(block_rows(), BF16), jnp.asarray(pool_rows().T, BF16), base, frac, frames, tail, cot)
    return outs[:5]


def finish_kernel(fine, terms, other, got, rows_of, grad_a, grad_b, ready, table, done):
    second = pltpu.make_async_copy(terms, grad_b, done.at[TILES // GROUP])
    second.start()
    load = pltpu.make_async_copy(rows_of, table, done.at[TILES // GROUP + 1])
    load.start()
    load.wait()
    copies = []
    for g in range(TILES // GROUP):
        for n in range(g * GROUP, (g + 1) * GROUP):
            value = dot(fine[n], got[table[GOT, n]]) * (1.0 / 16.0)
            ready[n] = (value + other[n].astype(F32)).astype(BF16)
        rows = pl.ds(g * GROUP, GROUP)
        copies.append(pltpu.make_async_copy(ready.at[rows], grad_a.at[rows], done.at[g]))
        copies[-1].start()
    for copy in copies:
        copy.wait()
    second.wait()


GROUP = 4


def finish(*parts):
    vmem = pl.BlockSpec(memory_space=pltpu.VMEM)
    out = jax.ShapeDtypeStruct((TILES, PIX, PIX), BF16)
    return pl.pallas_call(
        finish_kernel,
        in_specs=[vmem] * 5,
        out_specs=[pl.BlockSpec(memory_space=pl.ANY)] * 2,
        out_shape=[out, out],
        scratch_shapes=[
            pltpu.VMEM((TILES, PIX, PIX), BF16), pltpu.SMEM((8, SLOTS), jnp.int32),
            pltpu.SemaphoreType.DMA((TILES // GROUP + 2,))],
        compiler_params=pltpu.CompilerParams(vmem_limit_bytes=12 * 2**20),
        name="finish",
    )(*parts)


def body(frames, tail, cotangent, window_base, window_frac, fine_owner, fine_local, coarse_owner, coarse_block):
    ids = [v.reshape(8, 128) for v in (fine_owner, fine_local, coarse_owner, coarse_block)]
    parts = exchange(ids, frames[0], tail, cotangent[0].transpose(0, 2, 1, 3), window_base[0], window_frac[0])
    grad_a, grad_b = finish(*parts)
    return grad_a[None], grad_b[None]


def solution(mesh):
    in_specs = (
        P("clip", "space", None, None),
        P("space", None, None),
        P("clip", "space", None, None, None),
        P("clip", "space", None, None, None),
        P("clip", "space", None, None, None),
        P("clip", None, None),
        P("clip", None),
        P("clip", None, None),
        P("clip", None),
    )
    out_specs = (P("clip", "space", None, None), P("clip", "space", None, None))
    return jax.shard_map(body, mesh=mesh, in_specs=in_specs, out_specs=out_specs, check_vma=False)
```

```python
import functools

import jax
import jax.numpy as jnp
import numpy as np
from jax import lax
from jax.experimental import pallas as pl
from jax.experimental.pallas import tpu as pltpu
from jax.sharding import PartitionSpec as P

MESH = pl.DeviceIdType.MESH
POOL = 4
SIDE = 16
WIN = 9
PIX = 256
HALF = PIX // 2
NX, NZ, NC = 4, 4, 2
BLK = 2
TILES = 32
SLOTS = 2 * TILES
F32 = jnp.float32
BF16 = jnp.bfloat16


def placement():
    spread = np.zeros((2 * WIN * SIDE, WIN * WIN), np.float32)
    for a in range(WIN):
        for k in range(WIN):
            spread[a * SIDE + k, a * WIN + k] = 1
            spread[WIN * SIDE + a * SIDE + k + 1, a * WIN + k] = 1
    return spread


def pool_rows():
    rows = np.zeros((SIDE, PIX), np.float32)
    for y in range(SIDE):
        for x in range(SIDE):
            rows[(y // POOL) * POOL + x // POOL, y * SIDE + x] = 1
    return rows


def block_rows():
    rows = np.zeros((PIX, PIX), np.float32)
    for ty in range(4):
        for tx in range(4):
            for a in range(4):
                for b in range(4):
                    rows[(ty * 4 + a) * 16 + tx * 4 + b, (ty * 4 + tx) * 16 + a * 4 + b] = 1
    return rows


def dot(a, b):
    return jnp.dot(a, b, preferred_element_type=F32)


def window_map(spread, cot, base, frac):
    placed = dot(spread, cot)
    rows = WIN * SIDE
    fx = frac[0:1].astype(F32)
    fy = frac[1:2].astype(F32)
    shape = (SIDE, PIX)
    ox = jnp.broadcast_to(base[0:1] - WIN // 2, shape)
    oy = jnp.broadcast_to(base[1:2] - WIN // 2, shape)
    across = (1.0 - fx) * placed[:rows] + fx * placed[rows:]
    groups = []
    for y in range(WIN + 1):
        value = None
        if y < WIN:
            value = (1.0 - fy) * across[y * SIDE : (y + 1) * SIDE]
        if y > 0:
            below = fy * across[(y - 1) * SIDE : y * SIDE]
            value = below if value is None else value + below
        groups.append(value)
    for step in (1, 2, 4):
        chosen = (ox & step) != 0
        groups = [jnp.where(chosen, pltpu.roll(g, step, 0), g) for g in groups]
    zero = jnp.zeros(shape, F32)
    for step in (1, 2, 4):
        chosen = (oy & step) != 0
        count = min(SIDE, len(groups) + step)
        groups = [
            jnp.where(
                chosen,
                groups[y - step] if y >= step else zero,
                groups[y] if y < len(groups) else zero,
            )
            for y in range(count)
        ]
    return jnp.concatenate(groups, axis=0).astype(BF16)


def make_table(owner_ref, local_ref, c_owner_ref, c_block_ref, out_ref):
    me = lax.axis_index("space")
    total = functools.partial(jnp.sum, keepdims=True)
    sub, lane = (lax.broadcasted_iota(jnp.int32, (TILES, TILES), n) for n in range(2))
    wide_sub, wide_lane = (lax.broadcasted_iota(jnp.int32, (TILES, SLOTS), n) for n in range(2))
    tall_sub, tall_lane = (lax.broadcasted_iota(jnp.int32, (SLOTS, TILES), n) for n in range(2))
    slot_sub, slot_lane = (lax.broadcasted_iota(jnp.int32, (SLOTS, SLOTS), n) for n in range(2))
    one = (sub == lane).astype(F32)
    row_of = lambda n: lax.broadcasted_iota(jnp.int32, (TILES, 128), n)
    per_row = 128 // TILES
    pick_row = (lax.broadcasted_iota(jnp.int32, (TILES, 8), 0) // per_row == lax.broadcasted_iota(jnp.int32, (TILES, 8), 1)).astype(F32)
    in_part = row_of(0) % per_row == row_of(1) // TILES
    fold = (lax.broadcasted_iota(jnp.int32, (128, TILES), 0) % TILES == lax.broadcasted_iota(jnp.int32, (128, TILES), 1)).astype(F32)

    def square(ref):
        rows = dot(pick_row, ref[...].astype(F32))
        return dot(jnp.where(in_part, rows, 0.0), fold).astype(jnp.int32)

    owner, local, c_owner, c_block = (square(r) for r in (owner_ref, local_ref, c_owner_ref, c_block_ref))
    flip = (((0,), (0,)), ((), ()))

    def turned(v):
        return lax.dot_general(v.astype(F32), one, flip, preferred_element_type=F32).astype(jnp.int32)

    def mine(v):
        row = total(jnp.where(sub == me, v, 0), axis=0)
        return row, total(jnp.where(lane == me, turned(v), 0), axis=1)

    def parts(v):
        return v // (NZ * NC), (v // NC) % NZ, v % NC

    own_row, own_col = mine(owner)
    same = own_row == own_col
    rank_row = total(jnp.where(same & (sub < lane), 1, 0), axis=0)
    rank_col = total(jnp.where(same & (lane < sub), 1, 0), axis=1)
    ox, oz, oc = parts(own_row)
    got_slot = jnp.where(rank_row == 0, (oz * NC + oc) * NX + ox, TILES + (ox * NC + oc) * NZ + oz)
    ox, oz, oc = parts(own_col)
    cross = (oc + me) % NC * 4
    ret_slot = jnp.where(rank_col == 0, ox * 8 + cross + oz, TILES + oz * 8 + cross + ox)
    filled = jnp.max(jnp.where(ret_slot == wide_lane, wide_sub, 0), axis=0, keepdims=True)

    ctile_row, ctile_col = (
        ((o % NC) * (NX * NZ) + o // NC) * BLK + b for o, b in zip(mine(c_owner), mine(c_block)))
    named = ctile_col == wide_lane
    pick_a = jnp.min(jnp.where(named, wide_sub, TILES), axis=0, keepdims=True)
    pick_b = jnp.max(jnp.where(named, wide_sub, -1), axis=0, keepdims=True)
    pick_b = jnp.where((pick_b == pick_a) | (pick_b < 0), TILES, pick_b)

    def asked(hit, ids, earlier, axis):
        seen = hit.astype(F32)
        before = dot(earlier, seen) if axis == 0 else dot(seen, earlier)
        out = []
        for k in range(2):
            chosen = hit & (before.astype(jnp.int32) == k)
            value = total(jnp.where(chosen, ids, 0), axis=axis)
            count = total(jnp.where(chosen, 1, 0), axis=axis)
            out.append((value, jnp.where(count > 0, value, TILES)))
        return out

    (_, key0_row), (_, key1_row) = asked(turned(owner) == me, turned(local), (lane < sub).astype(F32), 0)
    (ask0, key0), (ask1, key1) = asked(owner == me, local, (sub < lane).astype(F32), 1)
    px, pz, pc = parts(wide_sub)
    cross = (pc + me) % NC * 4
    served = total(jnp.where(wide_lane == px * 8 + cross + pz, ask0, 0), axis=0)
    served += total(jnp.where(wide_lane == TILES + pz * 8 + cross + px, ask1, 0), axis=0)
    key_row = total(jnp.where(wide_lane == (pz * NC + pc) * NX + px, key0, 0), axis=0)
    key_row += total(jnp.where(wide_lane == TILES + (px * NC + pc) * NZ + pz, key1, 0), axis=0)
    px, pz, pc = parts(tall_lane)
    key_col = total(jnp.where(tall_sub == (pz * NC + pc) * NX + px, key0_row, 0), axis=1)
    key_col += total(jnp.where(tall_sub == TILES + (px * NC + pc) * NZ + pz, key1_row, 0), axis=1)
    ahead = (key_row < key_col) | ((key_row == key_col) & (slot_lane < slot_sub))
    place = total(jnp.where(ahead, 1, 0), axis=1)
    order = total(jnp.where(place == slot_lane, slot_sub, 0), axis=0)
    first = total(jnp.where(key_col < slot_lane, 1, 0), axis=0)
    out_ref[...] = jnp.zeros((8, SLOTS), jnp.int32)
    rows = (served, filled, pick_a, pick_b, ctile_row, got_slot, order, first)
    tops = (TILES - 1, TILES - 1, TILES, TILES, SLOTS - 1, SLOTS - 1, SLOTS - 1, SLOTS)
    for row, (value, top) in enumerate(zip(rows, tops)):
        out_ref[row : row + 1, : value.shape[1]] = jnp.clip(value, 0, top)


SERVED, FILLED, PICK_A, PICK_B, CTILE, GOT, ORDER, FIRST = range(8)


def exchange_kernel(
    owner, local_id, c_owner, c_block, spread_ref, pool_ref, perm_ref, widen_ref, base, frac, frames, tail, cot_ref,
    fine, terms, other, got, rows_of, back, every, below_every, ret_a, ret_b, get_a, get_b,
    first, cot, tiles, slots, partial, sibling, raw, pbuf,
    up_a, down_a, up_b, down_b, up_c, down_c, up_d, down_d, red_a, red_b, mid_a, mid_b, last_a, last_b, coarse, running, table,
    send, recv, local
):
    scale = 1.0 / 16.0
    clip = lax.axis_index("clip")
    space = lax.axis_index("space")
    x = space // (NZ * NC)
    z = (space // NC) % NZ
    c = space % NC
    counts = {"remote": 0, "local": 0}

    def along_x(d, core=0):
        return (clip, (((x + d) % NX) * NZ + z) * NC + (c + core) % NC)

    def along_z(d, core=0):
        return (clip, (x * NZ + (z + d) % NZ) * NC + (c + core) % NC)

    def remote(src, dst, device):
        n = counts["remote"]
        counts["remote"] += 1
        return pltpu.make_async_remote_copy(
            src_ref=src, dst_ref=dst, send_sem=send.at[n], recv_sem=recv.at[n],
            device_id=device, device_id_type=MESH)

    def here(src, dst):
        n = counts["local"]
        counts["local"] += 1
        return pltpu.make_async_copy(src, dst, local.at[n])

    def start(copies):
        for copy in copies:
            copy.start()
        return copies

    def arrive(copies):
        for copy in copies:
            copy.wait_recv()

    load = start([here(frames, first.at[pl.ds(0, TILES)]), here(cot_ref, cot)])
    at_end = clip == 3
    below = ((clip + 3) % 4, space)
    move_tiles = remote(frames, tiles, below)
    end_tiles = here(tail, tiles)
    pool_tail = here(tail, slots.at[pl.ds(0, TILES)])

    @pl.when(at_end)
    def _():
        end_tiles.start()

    @pl.when(clip == 0)
    def _():
        pool_tail.start()

    barrier = pltpu.get_barrier_semaphore()
    greeted = [along_x(d, k) for d in range(1, NX) for k in range(NC)]
    greeted += [along_z(d, k) for d in range(1, NZ) for k in range(NC)]
    greeted += [along_x(0, 1), ((clip + 1) % 4, space)]
    for device in greeted:
        pl.semaphore_signal(barrier, inc=1, device_id=device, device_id_type=MESH)
    pl.semaphore_wait(barrier, len(greeted))

    sent = []

    @pl.when(clip > 0)
    def _():
        move_tiles.start()

    def pool(source, target):
        def one(n, carry):
            for t in range(8):
                m = n * 8 + t
                rows = pl.ds(pl.multiple_of((m % 16) * SIDE, SIDE), SIDE)
                raw[m // 16, rows, :] = (dot(pool_ref[...], source[m]) * scale).astype(BF16)
            return carry
        lax.fori_loop(0, TILES // 8, one, 0)
        for b in range(BLK):
            target[b] = dot(perm_ref[...], raw[b]).astype(BF16)

    def products(begin, end, level, keep, put):
        def one(n, carry):
            for q in (2 * n, 2 * n + 1):
                weights = window_map(spread_ref[...], cot[q, :, level], base[q, level], frac[q, level])
                put[q] = (dot(weights, first[q]) * scale).astype(BF16)
                keep[q] = weights.T
            return carry
        lax.fori_loop(begin // 2, end // 2, one, 0)

    load[0].wait()

    @pl.when(clip > 0)
    def _():
        pool(first, pbuf)

    @pl.when(clip == 0)
    def _():
        pool_tail.wait()
        pool(slots, pbuf)

    top, bottom = pl.ds(0, HALF), pl.ds(HALF, HALF)
    keep_pool = start([here(pbuf, every.at[c, x, z])])
    pool_a1 = start([remote(pbuf.at[:, top], every.at[c, x, z, :, top], along_x(d)) for d in (2, 1, 3)])
    pool_b1 = start([remote(pbuf.at[:, bottom], every.at[c, x, z, :, bottom], along_z(d)) for d in (2, 1, 3)])
    sent += pool_a1 + pool_b1

    make_table(owner, local_id, c_owner, c_block, rows_of)
    load_table = start([here(rows_of, table)])
    load[1].wait()
    products(0, TILES // 4, 0, fine, terms)
    load_table[0].wait()

    keep_pool[0].wait()
    arrive(pool_a1)
    line = every.at[c, :, z, :, top]
    pool_a2 = start([remote(line, line, along_z(d)) for d in (1, NZ - 1)])
    arrive(pool_b1)
    line = every.at[c, x, :, :, bottom]
    pool_b2 = start([remote(line, line, along_x(d)) for d in (1, NX - 1)])
    sent += pool_a2 + pool_b2

    products(TILES // 4, TILES, 0, fine, terms)

    def fill_slots(half, source, row):
        def one(n, carry):
            for t in range(4):
                m = half * TILES + n * 4 + t
                slots[m] = source[table[row, m]]
            return carry
        lax.fori_loop(0, TILES // 4, one, 0)

    def group(half, n, k):
        return slots.at[pl.ds(half * TILES + n * 8 + k * 4, 4)]

    def first_hop(source, row, into_a, into_b):
        a, b = [], []
        for half, into, at, along, hops in ((0, into_a, x, along_x, a), (1, into_b, z, along_z, b)):
            fill_slots(half, source, row)
            for k in range(NC):
                part = into.at[pl.ds(k * 4, 4), at]
                far = start([remote(group(half, (at + d) % 4, k), part, along(d)) for d in (2, 1, 3)])
                hops.append((far, start([here(group(half, at, k), part)])))
        return a, b

    def first_sent(hops):
        for far, _ in hops[0] + hops[1]:
            for copy in far:
                copy.wait_send()

    def second_hop(hops, from_a, from_b, into):
        into_a = into.at[pl.ds((z * NC + c) * 4, 4)]
        into_b = into.at[pl.ds(TILES + (x * NC + c) * 4, 4)]
        far, near = [], []
        for k in range(NC):
            for hop, source, target, at, along in (
                (hops[0][k], from_a, into_a, z, along_z), (hops[1][k], from_b, into_b, x, along_x)):
                hop[1][0].wait()
                arrive(hop[0])
                far += start([remote(source.at[k * 4 + (at + d) % 4], target, along(d, k)) for d in (2, 1, 3)])
                if k == 0:
                    near += start([here(source.at[at], target)])
                else:
                    far += start([remote(source.at[4 + at], target, along(0, 1))])
        return far, near

    ret_hops = first_hop(terms, FILLED, ret_a, ret_b)

    products(0, TILES // 2, 1, other, first)

    x_up, x_down, z_up, z_down = (x + 1) % NX, (x + NX - 1) % NX, (z + 1) % NZ, (z + NZ - 1) % NZ
    low, high = pl.ds(0, 2), pl.ds(2, 2)
    arrive(pool_a2)
    line_up, line_down = every.at[c, low, z_down, :, top], every.at[c, high, z_up, :, top]
    pool_a3 = start([remote(line_up, line_up, along_z(1)), remote(line_down, line_down, along_z(NZ - 1))])
    arrive(pool_b2)
    line_up, line_down = every.at[c, x_down, low, :, bottom], every.at[c, x_up, high, :, bottom]
    pool_b3 = start([remote(line_up, line_up, along_x(1)), remote(line_down, line_down, along_x(NX - 1))])
    sent += pool_a3 + pool_b3

    products(TILES // 2, TILES, 1, other, first)
    first[TILES] = jnp.zeros((PIX, PIX), BF16)

    def fill(which, core):
        def one(n, carry):
            for t in range(4):
                m = 4 * n + t
                value = first[table[PICK_A, core * TILES + m]].astype(F32)
                value = value + first[table[PICK_B, core * TILES + m]].astype(F32)
                partial[which, m // (NZ * BLK), (m // BLK) % NZ, m % BLK] = value.astype(BF16)
            return carry
        lax.fori_loop(0, TILES // 4, one, 0)

    fill(1, 1 - c)
    share = start([remote(partial.at[1], sibling, along_x(0, 1))])
    fill(0, c)
    arrive(share)

    def join(n, carry):
        for t in range(4):
            m = 4 * n + t
            at = (m // (NZ * BLK), (m // BLK) % NZ, m % BLK)
            mine = partial[(0, *at)].astype(F32)
            partial[(0, *at)] = (mine + sibling[at].astype(F32)).astype(BF16)
        return carry

    lax.fori_loop(0, TILES // 4, join, 0)

    mine = partial.at[0]
    z_far, x_far = (z + 2) % NZ, (x + 2) % NX
    red_1 = start([
        remote(mine.at[low, z_far, :, top], up_a, along_z(1)),
        remote(mine.at[high, z_far, :, top], down_a, along_z(NZ - 1)),
        remote(mine.at[x_far, low, :, bottom], up_b, along_x(1)),
        remote(mine.at[x_far, high, :, bottom], down_b, along_x(NX - 1)),
    ])
    arrive(red_1)

    def pass_on(n, carry):
        i, b = n // BLK, n % BLK
        for at, extra in (
            ((0, i, z_up, b, top), up_a), ((0, i + 2, z_down, b, top), down_a),
            ((0, x_up, i, b, bottom), up_b), ((0, x_down, i + 2, b, bottom), down_b),
        ):
            partial[at] = (partial[at].astype(F32) + extra[i, b].astype(F32)).astype(BF16)
        return carry

    lax.fori_loop(0, 2 * BLK, pass_on, 0)
    red_2 = start([
        remote(mine.at[:, z_up, :, top], red_a.at[0], along_z(1)),
        remote(mine.at[:, z_down, :, top], red_a.at[1], along_z(NZ - 1)),
        remote(mine.at[x_up, :, :, bottom], red_b.at[0], along_x(1)),
        remote(mine.at[x_down, :, :, bottom], red_b.at[1], along_x(NX - 1)),
    ])

    arrive(pool_a3)
    arrive(pool_b3)
    pool_4 = start([remote(every.at[c], below_every.at[c], below)])

    ret_far, stay = second_hop(ret_hops, ret_a, ret_b, back)
    sent += ret_far

    arrive(red_2)

    def middle(n, carry):
        i, b = n // BLK, n % BLK
        for at, extra, into in (((0, i, z, b, top), red_a, mid_a), ((0, x, i, b, bottom), red_b, mid_b)):
            value = partial[at].astype(F32) + extra[0, i, b].astype(F32) + extra[1, i, b].astype(F32)
            into[i, b] = value.astype(BF16)
        return carry

    lax.fori_loop(0, NX * BLK, middle, 0)
    red_3 = start([
        remote(mid_a.at[x_far, 0], up_c, along_x(1)),
        remote(mid_a.at[x_far, 1], down_c, along_x(NX - 1)),
        remote(mid_b.at[z_far, 0], up_d, along_z(1)),
        remote(mid_b.at[z_far, 1], down_d, along_z(NZ - 1)),
    ])

    first_sent(ret_hops)

    @pl.when(at_end)
    def _():
        end_tiles.wait()

    @pl.when(clip < 3)
    def _():
        move_tiles.wait_recv()

    get_hops = first_hop(tiles, SERVED, get_a, get_b)

    arrive(red_3)
    for buffer, at, extra in (
        (mid_a, (x_up, 0), up_c), (mid_a, (x_down, 1), down_c),
        (mid_b, (z_up, 0), up_d), (mid_b, (z_down, 1), down_d),
    ):
        buffer[at] = (buffer[at].astype(F32) + extra[...].astype(F32)).astype(BF16)
    red_4 = start([
        remote(mid_a.at[x_up], last_a.at[0], along_x(1)),
        remote(mid_a.at[x_down], last_a.at[1], along_x(NX - 1)),
        remote(mid_b.at[z_up], last_b.at[0], along_z(1)),
        remote(mid_b.at[z_down], last_b.at[1], along_z(NZ - 1)),
    ])
    sent += red_3 + red_4

    get_far, near = second_hop(get_hops, get_a, get_b, got)
    sent += get_far

    arrive(red_4)
    for b in range(BLK):
        for rows, buffer, at, extra in ((top, mid_a, x, last_a), (bottom, mid_b, z, last_b)):
            value = buffer[at, b].astype(F32) + extra[0, b].astype(F32) + extra[1, b].astype(F32)
            coarse[b, rows] = value.astype(BF16)
    flip = (((0,), (0,)), ((), ()))
    for b in range(BLK):
        raw[b] = lax.dot_general(perm_ref[...], coarse[b], flip, preferred_element_type=F32).astype(BF16)

    arrive(ret_far)
    first_sent(get_hops)
    for copy in stay:
        copy.wait()
    load_back = start([here(back, slots)])
    load_back[0].wait()
    for part in range(4):
        rows = pl.ds(part * 64, 64)
        running[0] = jnp.zeros((64, PIX), F32)

        def add(n, value):
            for m in (4 * n, 4 * n + 1, 4 * n + 2, 4 * n + 3):
                value = value + slots[table[ORDER, m], rows].astype(F32)
                running[m + 1] = value
            return value

        lax.fori_loop(0, SLOTS // 4, add, jnp.zeros((64, PIX), F32))

        def gradient(n, carry):
            for t in range(8):
                m = 8 * n + t
                at = pl.ds(pl.multiple_of((m % 16) * SIDE, SIDE), SIDE)
                value = dot(widen_ref[rows], raw[m // 16, at]) * scale
                value = value + (running[table[FIRST, m + 1]] - running[table[FIRST, m]])
                terms[m, rows] = value.astype(BF16)
            return carry

        lax.fori_loop(0, TILES // 8, gradient, 0)

    arrive(pool_4)
    pool_5 = start([remote(below_every.at[c], below_every.at[c], along_x(0, 1))])
    sent += pool_4 + pool_5
    for copy in share + red_1 + red_2:
        copy.wait_send()
    arrive(pool_5)
    load_every = start([here(below_every, partial)])
    load_every[0].wait()

    def query(n, carry):
        for t in range(4):
            m = 4 * n + t
            at = table[CTILE, m]
            tile = partial[at // (NX * NZ * BLK), (at // (NZ * BLK)) % NX, (at // BLK) % NZ, at % BLK]
            other[m] = (dot(other[m], tile) * scale).astype(BF16)
        return carry

    lax.fori_loop(0, TILES // 4, query, 0)

    arrive(get_far)
    for copy in near:
        copy.wait()
    for copy in sent:
        copy.wait_send()

    @pl.when(clip > 0)
    def _():
        move_tiles.wait_send()


def exchange(ids, frames, tail, cot, base, frac):
    vmem = pl.BlockSpec(memory_space=pltpu.VMEM)
    hbm = pl.BlockSpec(memory_space=pl.ANY)
    tile = (PIX, PIX)
    shape = lambda *s: jax.ShapeDtypeStruct(s + tile, BF16)
    half = lambda *s: pltpu.VMEM(s + (HALF, PIX), BF16)
    full = lambda *s: pltpu.VMEM(s + tile, BF16)
    outs = pl.pallas_call(
        exchange_kernel,
        in_specs=[vmem] * 10 + [hbm] * 3,
        out_specs=[vmem] * 5 + [hbm] * 7,
        out_shape=[
            full(TILES), full(TILES), full(TILES), full(SLOTS),
            pltpu.VMEM((8, SLOTS), jnp.int32), shape(SLOTS), shape(NC, NX, NZ, BLK), shape(NC, NX, NZ, BLK),
            shape(8, NX), shape(8, NZ), shape(8, NX), shape(8, NZ),
        ],
        scratch_shapes=[
            full(TILES + 1), pltpu.VMEM((TILES, WIN * WIN, 2, PIX), BF16),
            full(TILES), full(SLOTS),
            full(2, NX, NZ, BLK), full(NX, NZ, BLK), full(BLK), full(BLK),
            half(2, BLK), half(2, BLK), half(2, BLK), half(2, BLK), half(), half(), half(), half(),
            half(2, NX, BLK), half(2, NZ, BLK), half(NX, BLK), half(NZ, BLK),
            half(2, BLK), half(2, BLK), full(BLK), pltpu.VMEM((SLOTS + 1, 64, PIX), F32),
            pltpu.SMEM((8, SLOTS), jnp.int32),
            pltpu.SemaphoreType.DMA((100,)), pltpu.SemaphoreType.DMA((100,)),
            pltpu.SemaphoreType.DMA((32,)),
        ],
        compiler_params=pltpu.CompilerParams(
            collective_id=0, has_side_effects=True, vmem_limit_bytes=43 * 2**20),
        name="exchange",
    )(*ids, jnp.asarray(placement(), BF16), jnp.asarray(pool_rows(), BF16),
      jnp.asarray(block_rows(), BF16), jnp.asarray(pool_rows().T, BF16), base, frac, frames, tail, cot)
    return outs[:5]


def finish_kernel(fine, terms, other, got, rows_of, grad_a, grad_b, ready, table, done):
    second = pltpu.make_async_copy(terms, grad_b, done.at[TILES // GROUP])
    second.start()
    load = pltpu.make_async_copy(rows_of, table, done.at[TILES // GROUP + 1])
    load.start()
    load.wait()
    copies = []
    for g in range(TILES // GROUP):
        for n in range(g * GROUP, (g + 1) * GROUP):
            value = dot(fine[n], got[table[GOT, n]]) * (1.0 / 16.0)
            ready[n] = (value + other[n].astype(F32)).astype(BF16)
        rows = pl.ds(g * GROUP, GROUP)
        copies.append(pltpu.make_async_copy(ready.at[rows], grad_a.at[rows], done.at[g]))
        copies[-1].start()
    for copy in copies:
        copy.wait()
    second.wait()


GROUP = 4


def finish(*parts):
    vmem = pl.BlockSpec(memory_space=pltpu.VMEM)
    out = jax.ShapeDtypeStruct((TILES, PIX, PIX), BF16)
    return pl.pallas_call(
        finish_kernel,
        in_specs=[vmem] * 5,
        out_specs=[pl.BlockSpec(memory_space=pl.ANY)] * 2,
        out_shape=[out, out],
        scratch_shapes=[
            pltpu.VMEM((TILES, PIX, PIX), BF16), pltpu.SMEM((8, SLOTS), jnp.int32),
            pltpu.SemaphoreType.DMA((TILES // GROUP + 2,))],
        compiler_params=pltpu.CompilerParams(vmem_limit_bytes=12 * 2**20),
        name="finish",
    )(*parts)


def body(frames, tail, cotangent, window_base, window_frac, fine_owner, fine_local, coarse_owner, coarse_block):
    ids = [v.reshape(8, 128) for v in (fine_owner, fine_local, coarse_owner, coarse_block)]
    parts = exchange(ids, frames[0], tail, cotangent[0].transpose(0, 2, 1, 3), window_base[0], window_frac[0])
    grad_a, grad_b = finish(*parts)
    return grad_a[None], grad_b[None]


def solution(mesh):
    in_specs = (
        P("clip", "space", None, None),
        P("space", None, None),
        P("clip", "space", None, None, None),
        P("clip", "space", None, None, None),
        P("clip", "space", None, None, None),
        P("clip", None, None),
        P("clip", None),
        P("clip", None, None),
        P("clip", None),
    )
    out_specs = (P("clip", "space", None, None), P("clip", "space", None, None))
    return jax.shard_map(body, mesh=mesh, in_specs=in_specs, out_specs=out_specs, check_vma=False)
```

```python
import functools

import jax
import jax.numpy as jnp
import numpy as np
from jax import lax
from jax.experimental import pallas as pl
from jax.experimental.pallas import tpu as pltpu
from jax.sharding import PartitionSpec as P

MESH = pl.DeviceIdType.MESH
POOL = 4
SIDE = 16
WIN = 9
PIX = 256
HALF = PIX // 2
NX, NZ, NC = 4, 4, 2
BLK = 2
TILES = 32
SLOTS = 2 * TILES
F32 = jnp.float32
BF16 = jnp.bfloat16


def placement():
    spread = np.zeros((2 * WIN * SIDE, WIN * WIN), np.float32)
    for a in range(WIN):
        for k in range(WIN):
            spread[a * SIDE + k, a * WIN + k] = 1
            spread[WIN * SIDE + a * SIDE + k + 1, a * WIN + k] = 1
    return spread


def pool_rows():
    rows = np.zeros((SIDE, PIX), np.float32)
    for y in range(SIDE):
        for x in range(SIDE):
            rows[(y // POOL) * POOL + x // POOL, y * SIDE + x] = 1
    return rows


def block_rows():
    rows = np.zeros((PIX, PIX), np.float32)
    for ty in range(4):
        for tx in range(4):
            for a in range(4):
                for b in range(4):
                    rows[(ty * 4 + a) * 16 + tx * 4 + b, (ty * 4 + tx) * 16 + a * 4 + b] = 1
    return rows


def dot(a, b):
    return jnp.dot(a, b, preferred_element_type=F32)


def window_map(spread, cot, base, frac):
    placed = dot(spread, cot)
    rows = WIN * SIDE
    fx = frac[0:1].astype(F32)
    fy = frac[1:2].astype(F32)
    shape = (SIDE, PIX)
    ox = jnp.broadcast_to(base[0:1] - WIN // 2, shape)
    oy = jnp.broadcast_to(base[1:2] - WIN // 2, shape)
    across = (1.0 - fx) * placed[:rows] + fx * placed[rows:]
    groups = []
    for y in range(WIN + 1):
        value = None
        if y < WIN:
            value = (1.0 - fy) * across[y * SIDE : (y + 1) * SIDE]
        if y > 0:
            below = fy * across[(y - 1) * SIDE : y * SIDE]
            value = below if value is None else value + below
        groups.append(value)
    for step in (1, 2, 4):
        chosen = (ox & step) != 0
        groups = [jnp.where(chosen, pltpu.roll(g, step, 0), g) for g in groups]
    zero = jnp.zeros(shape, F32)
    for step in (1, 2, 4):
        chosen = (oy & step) != 0
        count = min(SIDE, len(groups) + step)
        groups = [
            jnp.where(
                chosen,
                groups[y - step] if y >= step else zero,
                groups[y] if y < len(groups) else zero,
            )
            for y in range(count)
        ]
    return jnp.concatenate(groups, axis=0).astype(BF16)


def make_table(owner_ref, local_ref, c_owner_ref, c_block_ref, out_ref):
    me = lax.axis_index("space")
    total = functools.partial(jnp.sum, keepdims=True)
    sub, lane = (lax.broadcasted_iota(jnp.int32, (TILES, TILES), n) for n in range(2))
    wide_sub, wide_lane = (lax.broadcasted_iota(jnp.int32, (TILES, SLOTS), n) for n in range(2))
    tall_sub, tall_lane = (lax.broadcasted_iota(jnp.int32, (SLOTS, TILES), n) for n in range(2))
    slot_sub, slot_lane = (lax.broadcasted_iota(jnp.int32, (SLOTS, SLOTS), n) for n in range(2))
    one = (sub == lane).astype(F32)
    row_of = lambda n: lax.broadcasted_iota(jnp.int32, (TILES, 128), n)
    per_row = 128 // TILES
    pick_row = (lax.broadcasted_iota(jnp.int32, (TILES, 8), 0) // per_row == lax.broadcasted_iota(jnp.int32, (TILES, 8), 1)).astype(F32)
    in_part = row_of(0) % per_row == row_of(1) // TILES
    fold = (lax.broadcasted_iota(jnp.int32, (128, TILES), 0) % TILES == lax.broadcasted_iota(jnp.int32, (128, TILES), 1)).astype(F32)

    def square(ref):
        rows = dot(pick_row, ref[...].astype(F32))
        return dot(jnp.where(in_part, rows, 0.0), fold).astype(jnp.int32)

    owner, local, c_owner, c_block = (square(r) for r in (owner_ref, local_ref, c_owner_ref, c_block_ref))
    flip = (((0,), (0,)), ((), ()))

    def turned(v):
        return lax.dot_general(v.astype(F32), one, flip, preferred_element_type=F32).astype(jnp.int32)

    def mine(v):
        row = total(jnp.where(sub == me, v, 0), axis=0)
        return row, total(jnp.where(lane == me, turned(v), 0), axis=1)

    def parts(v):
        return v // (NZ * NC), (v // NC) % NZ, v % NC

    own_row, own_col = mine(owner)
    same = own_row == own_col
    rank_row = total(jnp.where(same & (sub < lane), 1, 0), axis=0)
    rank_col = total(jnp.where(same & (lane < sub), 1, 0), axis=1)
    ox, oz, oc = parts(own_row)
    got_slot = jnp.where(rank_row == 0, (oz * NC + oc) * NX + ox, TILES + (ox * NC + oc) * NZ + oz)
    ox, oz, oc = parts(own_col)
    cross = (oc + me) % NC * 4
    ret_slot = jnp.where(rank_col == 0, ox * 8 + cross + oz, TILES + oz * 8 + cross + ox)
    filled = jnp.max(jnp.where(ret_slot == wide_lane, wide_sub, 0), axis=0, keepdims=True)

    ctile_row, ctile_col = (
        ((o % NC) * (NX * NZ) + o // NC) * BLK + b for o, b in zip(mine(c_owner), mine(c_block)))
    named = ctile_col == wide_lane
    pick_a = jnp.min(jnp.where(named, wide_sub, TILES), axis=0, keepdims=True)
    pick_b = jnp.max(jnp.where(named, wide_sub, -1), axis=0, keepdims=True)
    pick_b = jnp.where((pick_b == pick_a) | (pick_b < 0), TILES, pick_b)

    def asked(hit, ids, earlier, axis):
        seen = hit.astype(F32)
        before = dot(earlier, seen) if axis == 0 else dot(seen, earlier)
        out = []
        for k in range(2):
            chosen = hit & (before.astype(jnp.int32) == k)
            value = total(jnp.where(chosen, ids, 0), axis=axis)
            count = total(jnp.where(chosen, 1, 0), axis=axis)
            out.append((value, jnp.where(count > 0, value, TILES)))
        return out

    (_, key0_row), (_, key1_row) = asked(turned(owner) == me, turned(local), (lane < sub).astype(F32), 0)
    (ask0, key0), (ask1, key1) = asked(owner == me, local, (sub < lane).astype(F32), 1)
    px, pz, pc = parts(wide_sub)
    cross = (pc + me) % NC * 4
    served = total(jnp.where(wide_lane == px * 8 + cross + pz, ask0, 0), axis=0)
    served += total(jnp.where(wide_lane == TILES + pz * 8 + cross + px, ask1, 0), axis=0)
    key_row = total(jnp.where(wide_lane == (pz * NC + pc) * NX + px, key0, 0), axis=0)
    key_row += total(jnp.where(wide_lane == TILES + (px * NC + pc) * NZ + pz, key1, 0), axis=0)
    px, pz, pc = parts(tall_lane)
    key_col = total(jnp.where(tall_sub == (pz * NC + pc) * NX + px, key0_row, 0), axis=1)
    key_col += total(jnp.where(tall_sub == TILES + (px * NC + pc) * NZ + pz, key1_row, 0), axis=1)
    ahead = (key_row < key_col) | ((key_row == key_col) & (slot_lane < slot_sub))
    place = total(jnp.where(ahead, 1, 0), axis=1)
    order = total(jnp.where(place == slot_lane, slot_sub, 0), axis=0)
    first = total(jnp.where(key_col < slot_lane, 1, 0), axis=0)
    out_ref[...] = jnp.zeros((8, SLOTS), jnp.int32)
    rows = (served, filled, pick_a, pick_b, ctile_row, got_slot, order, first)
    tops = (TILES - 1, TILES - 1, TILES, TILES, SLOTS - 1, SLOTS - 1, SLOTS - 1, SLOTS)
    for row, (value, top) in enumerate(zip(rows, tops)):
        out_ref[row : row + 1, : value.shape[1]] = jnp.clip(value, 0, top)


SERVED, FILLED, PICK_A, PICK_B, CTILE, GOT, ORDER, FIRST = range(8)


def exchange_kernel(
    owner, local_id, c_owner, c_block, spread_ref, pool_ref, perm_ref, widen_ref, base, frac, frames, tail, cot_ref,
    fine, terms, other, got, rows_of, back, every, below_every, ret_a, ret_b, get_a, get_b,
    first, cot, tiles, slots, partial, sibling, raw, pbuf,
    up_a, down_a, up_b, down_b, up_c, down_c, up_d, down_d, red_a, red_b, mid_a, mid_b, last_a, last_b, coarse, running, table,
    send, recv, local
):
    scale = 1.0 / 16.0
    clip = lax.axis_index("clip")
    space = lax.axis_index("space")
    x = space // (NZ * NC)
    z = (space // NC) % NZ
    c = space % NC
    counts = {"remote": 0, "local": 0}

    def along_x(d, core=0):
        return (clip, (((x + d) % NX) * NZ + z) * NC + (c + core) % NC)

    def along_z(d, core=0):
        return (clip, (x * NZ + (z + d) % NZ) * NC + (c + core) % NC)

    def remote(src, dst, device):
        n = counts["remote"]
        counts["remote"] += 1
        return pltpu.make_async_remote_copy(
            src_ref=src, dst_ref=dst, send_sem=send.at[n], recv_sem=recv.at[n],
            device_id=device, device_id_type=MESH)

    def here(src, dst):
        n = counts["local"]
        counts["local"] += 1
        return pltpu.make_async_copy(src, dst, local.at[n])

    def start(copies):
        for copy in copies:
            copy.start()
        return copies

    def arrive(copies):
        for copy in copies:
            copy.wait_recv()

    load = start([here(frames, first.at[pl.ds(0, TILES)]), here(cot_ref, cot)])
    at_end = clip == 3
    below = ((clip + 3) % 4, space)
    move_tiles = remote(frames, tiles, below)
    end_tiles = here(tail, tiles)
    pool_tail = here(tail, slots.at[pl.ds(0, TILES)])

    @pl.when(at_end)
    def _():
        end_tiles.start()

    @pl.when(clip == 0)
    def _():
        pool_tail.start()

    barrier = pltpu.get_barrier_semaphore()
    greeted = [along_x(d, k) for d in range(1, NX) for k in range(NC)]
    greeted += [along_z(d, k) for d in range(1, NZ) for k in range(NC)]
    greeted += [along_x(0, 1), ((clip + 1) % 4, space)]
    for device in greeted:
        pl.semaphore_signal(barrier, inc=1, device_id=device, device_id_type=MESH)
    def pool(source, target):
        def one(n, carry):
            for t in range(8):
                m = n * 8 + t
                rows = pl.ds(pl.multiple_of((m % 16) * SIDE, SIDE), SIDE)
                raw[m // 16, rows, :] = (dot(pool_ref[...], source[m]) * scale).astype(BF16)
            return carry
        lax.fori_loop(0, TILES // 8, one, 0)
        for b in range(BLK):
            target[b] = dot(perm_ref[...], raw[b]).astype(BF16)

    def products(begin, end, level, keep, put):
        def one(n, carry):
            for q in (2 * n, 2 * n + 1):
                weights = window_map(spread_ref[...], cot[q, :, level], base[q, level], frac[q, level])
                put[q] = (dot(weights, first[q]) * scale).astype(BF16)
                keep[q] = weights.T
            return carry
        lax.fori_loop(begin // 2, end // 2, one, 0)

    load[0].wait()

    @pl.when(clip > 0)
    def _():
        pool(first, pbuf)

    @pl.when(clip == 0)
    def _():
        pool_tail.wait()
        pool(slots, pbuf)

    pl.semaphore_wait(barrier, len(greeted))

    sent = []

    @pl.when(clip > 0)
    def _():
        move_tiles.start()

    top, bottom = pl.ds(0, HALF), pl.ds(HALF, HALF)
    keep_pool = start([here(pbuf, every.at[c, x, z])])
    pool_a1 = start([remote(pbuf.at[:, top], every.at[c, x, z, :, top], along_x(d)) for d in (2, 1, 3)])
    pool_b1 = start([remote(pbuf.at[:, bottom], every.at[c, x, z, :, bottom], along_z(d)) for d in (2, 1, 3)])
    sent += pool_a1 + pool_b1

    make_table(owner, local_id, c_owner, c_block, rows_of)
    load_table = start([here(rows_of, table)])
    load[1].wait()
    products(0, TILES // 4, 0, fine, terms)
    load_table[0].wait()

    keep_pool[0].wait()
    arrive(pool_a1)
    line = every.at[c, :, z, :, top]
    pool_a2 = start([remote(line, line, along_z(d)) for d in (1, NZ - 1)])
    arrive(pool_b1)
    line = every.at[c, x, :, :, bottom]
    pool_b2 = start([remote(line, line, along_x(d)) for d in (1, NX - 1)])
    sent += pool_a2 + pool_b2

    products(TILES // 4, TILES, 0, fine, terms)

    def fill_slots(half, source, row):
        def one(n, carry):
            for t in range(4):
                m = half * TILES + n * 4 + t
                slots[m] = source[table[row, m]]
            return carry
        lax.fori_loop(0, TILES // 4, one, 0)

    def group(half, n, k):
        return slots.at[pl.ds(half * TILES + n * 8 + k * 4, 4)]

    def first_hop(source, row, into_a, into_b):
        a, b = [], []
        for half, into, at, along, hops in ((0, into_a, x, along_x, a), (1, into_b, z, along_z, b)):
            fill_slots(half, source, row)
            for k in range(NC):
                part = into.at[pl.ds(k * 4, 4), at]
                far = start([remote(group(half, (at + d) % 4, k), part, along(d)) for d in (2, 1, 3)])
                hops.append((far, start([here(group(half, at, k), part)])))
        return a, b

    def first_sent(hops):
        for far, _ in hops[0] + hops[1]:
            for copy in far:
                copy.wait_send()

    def second_hop(hops, from_a, from_b, into):
        into_a = into.at[pl.ds((z * NC + c) * 4, 4)]
        into_b = into.at[pl.ds(TILES + (x * NC + c) * 4, 4)]
        far, near = [], []
        for k in range(NC):
            for hop, source, target, at, along in (
                (hops[0][k], from_a, into_a, z, along_z), (hops[1][k], from_b, into_b, x, along_x)):
                hop[1][0].wait()
                arrive(hop[0])
                far += start([remote(source.at[k * 4 + (at + d) % 4], target, along(d, k)) for d in (2, 1, 3)])
                if k == 0:
                    near += start([here(source.at[at], target)])
                else:
                    far += start([remote(source.at[4 + at], target, along(0, 1))])
        return far, near

    ret_hops = first_hop(terms, FILLED, ret_a, ret_b)

    products(0, TILES // 2, 1, other, first)

    x_up, x_down, z_up, z_down = (x + 1) % NX, (x + NX - 1) % NX, (z + 1) % NZ, (z + NZ - 1) % NZ
    low, high = pl.ds(0, 2), pl.ds(2, 2)
    arrive(pool_a2)
    line_up, line_down = every.at[c, low, z_down, :, top], every.at[c, high, z_up, :, top]
    pool_a3 = start([remote(line_up, line_up, along_z(1)), remote(line_down, line_down, along_z(NZ - 1))])
    arrive(pool_b2)
    line_up, line_down = every.at[c, x_down, low, :, bottom], every.at[c, x_up, high, :, bottom]
    pool_b3 = start([remote(line_up, line_up, along_x(1)), remote(line_down, line_down, along_x(NX - 1))])
    sent += pool_a3 + pool_b3

    products(TILES // 2, TILES, 1, other, first)
    first[TILES] = jnp.zeros((PIX, PIX), BF16)

    def fill(which, core):
        def one(n, carry):
            for t in range(4):
                m = 4 * n + t
                value = first[table[PICK_A, core * TILES + m]].astype(F32)
                value = value + first[table[PICK_B, core * TILES + m]].astype(F32)
                partial[which, m // (NZ * BLK), (m // BLK) % NZ, m % BLK] = value.astype(BF16)
            return carry
        lax.fori_loop(0, TILES // 4, one, 0)

    fill(1, 1 - c)
    share = start([remote(partial.at[1], sibling, along_x(0, 1))])
    fill(0, c)
    arrive(share)

    def join(n, carry):
        for t in range(4):
            m = 4 * n + t
            at = (m // (NZ * BLK), (m // BLK) % NZ, m % BLK)
            mine = partial[(0, *at)].astype(F32)
            partial[(0, *at)] = (mine + sibling[at].astype(F32)).astype(BF16)
        return carry

    lax.fori_loop(0, TILES // 4, join, 0)

    mine = partial.at[0]
    z_far, x_far = (z + 2) % NZ, (x + 2) % NX
    red_1 = start([
        remote(mine.at[low, z_far, :, top], up_a, along_z(1)),
        remote(mine.at[high, z_far, :, top], down_a, along_z(NZ - 1)),
        remote(mine.at[x_far, low, :, bottom], up_b, along_x(1)),
        remote(mine.at[x_far, high, :, bottom], down_b, along_x(NX - 1)),
    ])
    arrive(red_1)

    def pass_on(n, carry):
        i, b = n // BLK, n % BLK
        for at, extra in (
            ((0, i, z_up, b, top), up_a), ((0, i + 2, z_down, b, top), down_a),
            ((0, x_up, i, b, bottom), up_b), ((0, x_down, i + 2, b, bottom), down_b),
        ):
            partial[at] = (partial[at].astype(F32) + extra[i, b].astype(F32)).astype(BF16)
        return carry

    lax.fori_loop(0, 2 * BLK, pass_on, 0)
    red_2 = start([
        remote(mine.at[:, z_up, :, top], red_a.at[0], along_z(1)),
        remote(mine.at[:, z_down, :, top], red_a.at[1], along_z(NZ - 1)),
        remote(mine.at[x_up, :, :, bottom], red_b.at[0], along_x(1)),
        remote(mine.at[x_down, :, :, bottom], red_b.at[1], along_x(NX - 1)),
    ])

    arrive(pool_a3)
    arrive(pool_b3)
    pool_4 = start([remote(every.at[c], below_every.at[c], below)])

    ret_far, stay = second_hop(ret_hops, ret_a, ret_b, back)
    sent += ret_far

    arrive(red_2)

    def middle(n, carry):
        i, b = n // BLK, n % BLK
        for at, extra, into in (((0, i, z, b, top), red_a, mid_a), ((0, x, i, b, bottom), red_b, mid_b)):
            value = partial[at].astype(F32) + extra[0, i, b].astype(F32) + extra[1, i, b].astype(F32)
            into[i, b] = value.astype(BF16)
        return carry

    lax.fori_loop(0, NX * BLK, middle, 0)
    red_3 = start([
        remote(mid_a.at[x_far, 0], up_c, along_x(1)),
        remote(mid_a.at[x_far, 1], down_c, along_x(NX - 1)),
        remote(mid_b.at[z_far, 0], up_d, along_z(1)),
        remote(mid_b.at[z_far, 1], down_d, along_z(NZ - 1)),
    ])

    first_sent(ret_hops)

    @pl.when(at_end)
    def _():
        end_tiles.wait()

    @pl.when(clip < 3)
    def _():
        move_tiles.wait_recv()

    get_hops = first_hop(tiles, SERVED, get_a, get_b)

    arrive(red_3)
    for buffer, at, extra in (
        (mid_a, (x_up, 0), up_c), (mid_a, (x_down, 1), down_c),
        (mid_b, (z_up, 0), up_d), (mid_b, (z_down, 1), down_d),
    ):
        buffer[at] = (buffer[at].astype(F32) + extra[...].astype(F32)).astype(BF16)
    red_4 = start([
        remote(mid_a.at[x_up], last_a.at[0], along_x(1)),
        remote(mid_a.at[x_down], last_a.at[1], along_x(NX - 1)),
        remote(mid_b.at[z_up], last_b.at[0], along_z(1)),
        remote(mid_b.at[z_down], last_b.at[1], along_z(NZ - 1)),
    ])
    sent += red_3 + red_4

    get_far, near = second_hop(get_hops, get_a, get_b, got)
    sent += get_far

    arrive(red_4)
    for b in range(BLK):
        for rows, buffer, at, extra in ((top, mid_a, x, last_a), (bottom, mid_b, z, last_b)):
            value = buffer[at, b].astype(F32) + extra[0, b].astype(F32) + extra[1, b].astype(F32)
            coarse[b, rows] = value.astype(BF16)
    flip = (((0,), (0,)), ((), ()))
    for b in range(BLK):
        raw[b] = lax.dot_general(perm_ref[...], coarse[b], flip, preferred_element_type=F32).astype(BF16)

    arrive(ret_far)
    first_sent(get_hops)
    for copy in stay:
        copy.wait()
    load_back = start([here(back, slots)])
    load_back[0].wait()
    for part in range(4):
        rows = pl.ds(part * 64, 64)
        running[0] = jnp.zeros((64, PIX), F32)

        def add(n, value):
            for m in (4 * n, 4 * n + 1, 4 * n + 2, 4 * n + 3):
                value = value + slots[table[ORDER, m], rows].astype(F32)
                running[m + 1] = value
            return value

        lax.fori_loop(0, SLOTS // 4, add, jnp.zeros((64, PIX), F32))

        def gradient(n, carry):
            for t in range(8):
                m = 8 * n + t
                at = pl.ds(pl.multiple_of((m % 16) * SIDE, SIDE), SIDE)
                value = dot(widen_ref[rows], raw[m // 16, at]) * scale
                value = value + (running[table[FIRST, m + 1]] - running[table[FIRST, m]])
                terms[m, rows] = value.astype(BF16)
            return carry

        lax.fori_loop(0, TILES // 8, gradient, 0)

    arrive(pool_4)
    pool_5 = start([remote(below_every.at[c], below_every.at[c], along_x(0, 1))])
    sent += pool_4 + pool_5
    for copy in share + red_1 + red_2:
        copy.wait_send()
    arrive(pool_5)
    load_every = start([here(below_every, partial)])
    load_every[0].wait()

    def query(n, carry):
        for t in range(4):
            m = 4 * n + t
            at = table[CTILE, m]
            tile = partial[at // (NX * NZ * BLK), (at // (NZ * BLK)) % NX, (at // BLK) % NZ, at % BLK]
            other[m] = (dot(other[m], tile) * scale).astype(BF16)
        return carry

    lax.fori_loop(0, TILES // 4, query, 0)

    arrive(get_far)
    for copy in near:
        copy.wait()
    for copy in sent:
        copy.wait_send()

    @pl.when(clip > 0)
    def _():
        move_tiles.wait_send()


def exchange(ids, frames, tail, cot, base, frac):
    vmem = pl.BlockSpec(memory_space=pltpu.VMEM)
    hbm = pl.BlockSpec(memory_space=pl.ANY)
    tile = (PIX, PIX)
    shape = lambda *s: jax.ShapeDtypeStruct(s + tile, BF16)
    half = lambda *s: pltpu.VMEM(s + (HALF, PIX), BF16)
    full = lambda *s: pltpu.VMEM(s + tile, BF16)
    outs = pl.pallas_call(
        exchange_kernel,
        in_specs=[vmem] * 10 + [hbm] * 3,
        out_specs=[vmem] * 5 + [hbm] * 7,
        out_shape=[
            full(TILES), full(TILES), full(TILES), full(SLOTS),
            pltpu.VMEM((8, SLOTS), jnp.int32), shape(SLOTS), shape(NC, NX, NZ, BLK), shape(NC, NX, NZ, BLK),
            shape(8, NX), shape(8, NZ), shape(8, NX), shape(8, NZ),
        ],
        scratch_shapes=[
            full(TILES + 1), pltpu.VMEM((TILES, WIN * WIN, 2, PIX), BF16),
            full(TILES), full(SLOTS),
            full(2, NX, NZ, BLK), full(NX, NZ, BLK), full(BLK), full(BLK),
            half(2, BLK), half(2, BLK), half(2, BLK), half(2, BLK), half(), half(), half(), half(),
            half(2, NX, BLK), half(2, NZ, BLK), half(NX, BLK), half(NZ, BLK),
            half(2, BLK), half(2, BLK), full(BLK), pltpu.VMEM((SLOTS + 1, 64, PIX), F32),
            pltpu.SMEM((8, SLOTS), jnp.int32),
            pltpu.SemaphoreType.DMA((100,)), pltpu.SemaphoreType.DMA((100,)),
            pltpu.SemaphoreType.DMA((32,)),
        ],
        compiler_params=pltpu.CompilerParams(
            collective_id=0, has_side_effects=True, vmem_limit_bytes=43 * 2**20),
        name="exchange",
    )(*ids, jnp.asarray(placement(), BF16), jnp.asarray(pool_rows(), BF16),
      jnp.asarray(block_rows(), BF16), jnp.asarray(pool_rows().T, BF16), base, frac, frames, tail, cot)
    return outs[:5]


def finish_kernel(fine, terms, other, got, rows_of, grad_a, grad_b, ready, table, done):
    second = pltpu.make_async_copy(terms, grad_b, done.at[TILES // GROUP])
    second.start()
    load = pltpu.make_async_copy(rows_of, table, done.at[TILES // GROUP + 1])
    load.start()
    load.wait()
    copies = []
    for g in range(TILES // GROUP):
        for n in range(g * GROUP, (g + 1) * GROUP):
            value = dot(fine[n], got[table[GOT, n]]) * (1.0 / 16.0)
            ready[n] = (value + other[n].astype(F32)).astype(BF16)
        rows = pl.ds(g * GROUP, GROUP)
        copies.append(pltpu.make_async_copy(ready.at[rows], grad_a.at[rows], done.at[g]))
        copies[-1].start()
    for copy in copies:
        copy.wait()
    second.wait()


GROUP = 4


def finish(*parts):
    vmem = pl.BlockSpec(memory_space=pltpu.VMEM)
    out = jax.ShapeDtypeStruct((TILES, PIX, PIX), BF16)
    return pl.pallas_call(
        finish_kernel,
        in_specs=[vmem] * 5,
        out_specs=[pl.BlockSpec(memory_space=pl.ANY)] * 2,
        out_shape=[out, out],
        scratch_shapes=[
            pltpu.VMEM((TILES, PIX, PIX), BF16), pltpu.SMEM((8, SLOTS), jnp.int32),
            pltpu.SemaphoreType.DMA((TILES // GROUP + 2,))],
        compiler_params=pltpu.CompilerParams(vmem_limit_bytes=12 * 2**20),
        name="finish",
    )(*parts)


def body(frames, tail, cotangent, window_base, window_frac, fine_owner, fine_local, coarse_owner, coarse_block):
    ids = [v.reshape(8, 128) for v in (fine_owner, fine_local, coarse_owner, coarse_block)]
    parts = exchange(ids, frames[0], tail, cotangent[0].transpose(0, 2, 1, 3), window_base[0], window_frac[0])
    grad_a, grad_b = finish(*parts)
    return grad_a[None], grad_b[None]


def solution(mesh):
    in_specs = (
        P("clip", "space", None, None),
        P("space", None, None),
        P("clip", "space", None, None, None),
        P("clip", "space", None, None, None),
        P("clip", "space", None, None, None),
        P("clip", None, None),
        P("clip", None),
        P("clip", None, None),
        P("clip", None),
    )
    out_specs = (P("clip", "space", None, None), P("clip", "space", None, None))
    return jax.shard_map(body, mesh=mesh, in_specs=in_specs, out_specs=out_specs, check_vma=False)
```
